256 devices in a mesh: section: 8 (over x, y_hi), dp: 32 (over z, y_lo, core).
Axes of the slice: x: 4, y: 4 (y_hi: 2, y_lo: 2; y = y_hi * 2 + y_lo), z: 8, core: 2. Of those that a mesh axis runs over, the one named last changes fastest.
Arguments:
- train_acts: bfloat16 [8, 5888, 27648], P('section', 'dp'), may hold values from -6 to 6
- train_grads: bfloat16 [8, 5888, 5120], P('section', 'dp'), may hold values from -0.011962891 to 0.011962891
- train_ids: int32 [5888], P('dp'), may hold values from 0 to 255, as said below
- val_acts: bfloat16 [8, 256, 27648], P('section', 'dp'), may hold values from -6 to 6
- val_grads: bfloat16 [8, 256, 5120], P('section', 'dp'), may hold values from -0.011962891 to 0.011962891
- val_ids: int32 [256], P('dp'), may hold values from 0 to 15, never falling along the last dimension, each value on 1 to 32 neighbouring positions
Outputs:
- scores: float32 [256, 16], P('dp', 'section')
The draws below stay inside these ranges and needn't reach their ends.
Inputs may be any that keep to these rules, and one draw needn't show every extreme that they name: `train_ids`: the training tokens of rows k * 184 to (k + 1) * 184 - 1 belong to sequences k * 8 to (k + 1) * 8 - 1, in non-decreasing order, each of these sequences with one token or more. `val_ids`: validation sequence numbers never fall along the tokens; each sequence has 1 to 32 tokens.
All inputs are finite; a program needn't handle non-finite values.
Results may differ from the reference program's by a relative error of at most 0.0003.
Values may be sent and summed in bfloat16 or wider, within the bound.
No kernel may reach another device: no remote copies, remote signals or barrier semaphores. Data moves between devices by JAX's collectives and lax.ppermute only.
A program may use at most 128 MiB of HBM per device.

```python
import math
import jax
import jax.numpy as jnp
import numpy as np
from jax import lax

FF = 27648
D = 5120
TOK_DEV = 184
SEQ_DEV = 8
LAYERS = 8
TOKENS = 5888
TRAIN_SEQS = 256
VAL = 256
VAL_SEQS = 16
VAL_MOST = 32


def draw_train_ids(key, part):
    key = jax.random.fold_in(key, 7)
    blocks = TOKENS // TOK_DEV
    raw = jax.random.randint(key, (blocks, TOK_DEV - 1), 0, 1 << 20, dtype=jnp.int32)
    ranked = raw * TOK_DEV + jnp.arange(TOK_DEV - 1, dtype=jnp.int32)[None, :]
    order = jnp.argsort(ranked, axis=1, stable=True).astype(jnp.int32)
    chosen = order[:, :SEQ_DEV - 1] + 1
    places = jnp.arange(TOK_DEV, dtype=jnp.int32)
    starts = jnp.any(places[None, None, :] == chosen[:, :, None], axis=1).astype(jnp.int32)
    local_ids = jnp.cumsum(starts, axis=1).astype(jnp.int32)
    offsets = (jnp.arange(blocks, dtype=jnp.int32) * SEQ_DEV)[:, None]
    return (local_ids + offsets).reshape(-1).astype(jnp.int32)


def block_levels(stream_key, extent, pieces, least, largest):
    loudness, own = 1.0, jax.random.fold_in(stream_key, 6)
    for position, parts in pieces:
        heights = jnp.exp(jax.random.uniform(jax.random.fold_in(own, position), (parts,), jnp.float32, least / len(pieces), largest / len(pieces)))
        loudness = loudness * jnp.repeat(heights, extent[position] // parts).reshape([-1 if axis == position else 1 for axis in range(len(extent))])
    return loudness


def length_profile(number_of, total, limit, slope):
    loads = [(1 << 20) // math.isqrt(grade ** slope) + 1 for grade in range(2, number_of + 1)]
    spare, given = total - limit - (number_of - 1), [1] * (number_of - 1)
    while spare > 0:
        movable = [i for i in range(number_of - 1) if given[i] < limit]
        pool, budget = sum([loads[i] for i in movable]), spare
        for i in movable:
            more = min(limit - given[i], max(1, budget * loads[i] // pool), spare)
            given[i] = given[i] + more
            spare = spare - more
    return np.array([limit] + given)


def uneven_parts(key, number_of, total, bound, skew):
    if number_of == 2:
        one = jax.random.randint(key, (), max(1, total - bound), min(bound, total - 1) + 1)
        return jnp.stack([one, total - one])
    lengths = jnp.asarray(length_profile(number_of, total, bound, skew), jnp.int32)
    twos = (number_of - 1) // 2
    giver, taker = lengths[1:1 + 2 * twos:2], lengths[2:2 + 2 * twos:2]
    slack = jnp.minimum(giver - 1, bound - taker)
    shifted = jax.random.randint(jax.random.fold_in(key, 1), (twos,), 0, 1 << 20) % (slack + 1)
    lengths = lengths.at[1:1 + 2 * twos:2].set(giver - shifted).at[2:2 + 2 * twos:2].set(taker + shifted)
    return lengths[jax.random.permutation(jax.random.fold_in(key, 2), number_of)]


def centred(key, extent, width, reach, pieces=(), kind=jnp.bfloat16):
    values = width * jax.random.normal(key, extent, jnp.float32)
    if pieces:
        values = values * block_levels(key, extent, pieces, -0.22, 0.18)
    return jnp.clip(values, -reach, reach).astype(kind)


def setup_inputs(seed: int = 0) -> dict:
    keys = jax.random.split(jax.random.key(seed), 7)
    train_acts = centred(keys[0], (LAYERS, TOKENS, FF), 1.0, 6.0, ((0, 8), (1, 32)))
    train_grads = centred(keys[1], (LAYERS, TOKENS, D), 0.002, 0.011962891, ((0, 8), (1, 32)))
    train_ids = draw_train_ids(jax.random.fold_in(keys[6], 71), 0)
    val_acts = centred(keys[3], (LAYERS, VAL, FF), 1.0, 6.0, ((0, 8), (1, 32)))
    val_grads = centred(keys[4], (LAYERS, VAL, D), 0.002, 0.011962891, ((0, 8), (1, 32)))
    val_ids = jnp.searchsorted(jnp.cumsum(uneven_parts(keys[5], VAL_SEQS, VAL, VAL_MOST, 1)), jnp.arange(VAL), side="right").astype(jnp.int32)
    return dict(train_acts=train_acts, train_grads=train_grads, train_ids=train_ids, val_acts=val_acts, val_grads=val_grads, val_ids=val_ids)


def reference(train_acts, train_grads, train_ids, val_acts, val_grads, val_ids):
    train_onehot = (train_ids[:, None] == jnp.arange(TRAIN_SEQS, dtype=jnp.int32)[None, :]).astype(jnp.float32)
    val_onehot = (val_ids[:, None] == jnp.arange(VAL_SEQS, dtype=jnp.int32)[None, :]).astype(jnp.float32)
    scores_sum = jnp.zeros((TRAIN_SEQS, VAL_SEQS), jnp.float32)
    for layer_index in range(LAYERS):
        act_gram = jnp.dot(train_acts[layer_index], val_acts[layer_index].T, preferred_element_type=jnp.float32)
        grad_gram = jnp.dot(train_grads[layer_index], val_grads[layer_index].T, preferred_element_type=jnp.float32)
        hadamard = act_gram * grad_gram
        by_train = jnp.dot(train_onehot.T, hadamard, precision=lax.Precision.HIGHEST)
        scores_sum = scores_sum + jnp.dot(by_train, val_onehot, precision=lax.Precision.HIGHEST)
    return scores_sum
```

```python
import jax
import jax.numpy as jnp
from jax import lax
from jax.experimental import pallas as pl
from jax.experimental.pallas import tpu as pltpu
from jax.sharding import Mesh, PartitionSpec as P

SEQ_DEV = 8
VAL_SEQS = 16
LANES = 128
ACT_TILE = 1536
GRAD_TILE = 1280
F32 = jnp.float32
HIGHEST = lax.Precision.HIGHEST


def rows_of(blocks, start, size):
    parts = [block[:, pl.ds(start, size)].astype(F32) for block in blocks]
    return jnp.concatenate(parts, axis=0).astype(jnp.bfloat16)


def contract(left, piece):
    return lax.dot_general(left, piece, (((1,), (1,)), ((), ())), preferred_element_type=F32)


def train_onehots(ids_ref):
    places = lax.broadcasted_iota(jnp.int32, (2 * SEQ_DEV, ids_ref.shape[1]), 0)
    return [(ids_ref[k : k + 1, :] == places).astype(F32) for k in range(2)]


def val_onehot(blocks, start):
    width = blocks[0].shape[1]
    numbers = [block[:, width - LANES :].astype(F32)[:, :VAL_SEQS] for block in blocks]
    stacked = jnp.concatenate(numbers, axis=0)
    return (stacked == lax.broadcasted_iota(jnp.int32, stacked.shape, 1).astype(F32)).astype(F32)


def scores_of(onehots, act_grams, grad_grams, val_hot):
    total = None
    for hot, act, grad in zip(onehots, act_grams, grad_grams):
        term = jnp.dot(hot, act * grad, precision=HIGHEST, preferred_element_type=F32)
        total = term if total is None else total + term
    return jnp.dot(total, val_hot, precision=HIGHEST, preferred_element_type=F32)


def low_kernel(count, steps, epilogue, *refs):
    own, partner = refs[:2]
    blocks = refs[2 : 2 + count]
    rest, acc = refs[2 + count : -1], refs[-1]
    i = pl.program_id(0)

    @pl.when(i == 0)
    def _():
        acc[...] = jnp.zeros_like(acc)

    piece = rows_of(blocks, pl.multiple_of(i * ACT_TILE, LANES), ACT_TILE)
    acc[0] += contract(own[0], piece)
    acc[1] += contract(partner[0], piece)

    @pl.when(i == steps - 1)
    def _():
        epilogue(acc, *rest)


def high_kernel(count, act_steps, grad_steps, epilogue, *refs):
    own, partner, own_grads, partner_grads = refs[:4]
    blocks = refs[4 : 4 + count]
    rest, acc, accg = refs[4 + count : -2], refs[-2], refs[-1]
    i = pl.program_id(0)

    @pl.when(i == 0)
    def _():
        acc[...] = jnp.zeros_like(acc)
        accg[...] = jnp.zeros_like(accg)

    @pl.when(i < act_steps)
    def _():
        piece = rows_of(blocks, pl.multiple_of(i * ACT_TILE, LANES), ACT_TILE)
        acc[0] += contract(own[0], piece)
        acc[1] += contract(partner[0], piece)

    @pl.when(i >= act_steps)
    def _():
        start = act_steps * ACT_TILE + (i - act_steps) * GRAD_TILE
        piece = rows_of(blocks, pl.multiple_of(start, LANES), GRAD_TILE)
        accg[0] += contract(own_grads[0], piece)
        accg[1] += contract(partner_grads[0], piece)

    @pl.when(i == act_steps + grad_steps - 1)
    def _():
        epilogue(blocks, acc, accg, *rest)


def keep_low(acc, out):
    out[...] = acc[...]


def first_high(near, blocks, acc, accg, ids, low, score, act_out, grad_out, hot_out):
    split = SEQ_DEV * near
    acts = [acc[k] for k in range(2)]
    grads = [accg[k] for k in range(2)]
    score[...] = scores_of(
        train_onehots(ids),
        [acts[k][:, :split] + low[k] for k in range(2)],
        [grads[k][:, :split] for k in range(2)],
        val_onehot(blocks[:near], 0),
    )
    for k in range(2):
        act_out[k] = acts[k][:, split:]
        grad_out[k] = grads[k][:, split:]
    hot_out[...] = val_onehot(blocks[near:], 0)


def second_low(near, acc, ids, score_in, act_in, grad_in, hot_in, score, low_out):
    split = SEQ_DEV * near
    acts = [acc[k] for k in range(2)]
    score[...] = score_in[...] + scores_of(
        train_onehots(ids),
        [acts[k][:, :split] + act_in[k] for k in range(2)],
        [grad_in[k] for k in range(2)],
        hot_in[...],
    )
    for k in range(2):
        low_out[k] = acts[k][:, split:]


def last_high(blocks, acc, accg, ids, score_in, low, score):
    score[...] = score_in[...] + scores_of(
        train_onehots(ids),
        [acc[k] + low[k] for k in range(2)],
        [accg[k] for k in range(2)],
        val_onehot(blocks, 0),
    )


def vmem():
    return pl.BlockSpec(memory_space=pltpu.VMEM)


def params():
    return pltpu.CompilerParams(vmem_limit_bytes=40 * 1024 * 1024)


def call_low(epilogue, acts, blocks, extra, outs):
    tokens = acts[0].shape[1]
    steps = blocks[0].shape[1] // ACT_TILE
    spec = pl.BlockSpec((1, tokens, ACT_TILE), lambda i: (0, 0, i))
    rows = SEQ_DEV * len(blocks)
    return pl.pallas_call(
        lambda *refs: low_kernel(len(blocks), steps, epilogue, *refs),
        grid=(steps,),
        in_specs=[spec, spec] + [vmem()] * (len(blocks) + len(extra)),
        out_specs=[vmem()] * len(outs),
        out_shape=[jax.ShapeDtypeStruct(shape, F32) for shape in outs],
        scratch_shapes=[pltpu.VMEM((2, tokens, rows), F32)],
        compiler_params=params(),
        cost_estimate=pl.CostEstimate(
            flops=4 * tokens * 128 * steps * ACT_TILE,
            bytes_accessed=4 * tokens * steps * ACT_TILE,
            transcendentals=0,
        ),
    )(*acts, *blocks, *extra)


def call_high(epilogue, acts, grads, blocks, extra, outs):
    tokens = acts[0].shape[1]
    width = acts[0].shape[2]
    grad_width = grads[0].shape[2]
    act_steps = (blocks[0].shape[1] - grad_width - LANES) // ACT_TILE
    first = width // ACT_TILE - act_steps
    grad_steps = grad_width // GRAD_TILE
    spec = pl.BlockSpec(
        (1, tokens, ACT_TILE), lambda i: (0, 0, first + jnp.minimum(i, act_steps - 1))
    )
    grad_spec = pl.BlockSpec(
        (1, tokens, GRAD_TILE), lambda i: (0, 0, jnp.maximum(i - act_steps, 0))
    )
    rows = SEQ_DEV * len(blocks)
    return pl.pallas_call(
        lambda *refs: high_kernel(len(blocks), act_steps, grad_steps, epilogue, *refs),
        grid=(act_steps + grad_steps,),
        in_specs=[spec, spec, grad_spec, grad_spec] + [vmem()] * (len(blocks) + len(extra)),
        out_specs=[vmem()] * len(outs),
        out_shape=[jax.ShapeDtypeStruct(shape, F32) for shape in outs],
        scratch_shapes=[pltpu.VMEM((2, tokens, rows), F32)] * 2,
        compiler_params=params(),
        cost_estimate=pl.CostEstimate(
            flops=4 * tokens * 128 * (act_steps * ACT_TILE + grad_width),
            bytes_accessed=4 * tokens * (act_steps * ACT_TILE + grad_width),
            transcendentals=0,
        ),
    )(*acts, *grads, *blocks, *extra)


def on_device(train_acts, train_grads, train_ids, val_acts, val_grads, val_ids):
    width, tokens = train_acts.shape[2], train_acts.shape[1]
    cut = (width // ACT_TILE * 11 // 18) * ACT_TILE
    core = lax.axis_index("core")
    pair = lax.axis_index("zy")
    places = lax.axis_size("zy")
    sections = lax.axis_size("section")

    swap = [(0, 1), (1, 0)]
    up = [(i, (i + 2) % places) for i in range(places)]
    down = [(i, (i - 2) % places) for i in range(places)]
    across = [(i, i ^ 1) for i in range(places)]

    def ahead(block):
        return lax.ppermute(block, "zy", up)

    def back(block):
        return lax.ppermute(block, "zy", down)

    def beside(block):
        return lax.ppermute(block, "zy", across)

    numbers = jnp.broadcast_to(val_ids.astype(jnp.bfloat16)[:, None], (SEQ_DEV, LANES))
    low = {0: val_acts[0, :, :cut]}
    high = {0: jnp.concatenate([val_acts[0, :, cut:], val_grads[0], numbers], axis=1)}
    for held in (low, high):
        for d in (1, 2, 3):
            held[-d] = ahead(held[1 - d])
            held[d] = back(held[d - 1])
    low[4] = ahead(low[-3])
    high[4] = back(high[3])
    olow = {0: beside(low[0])}
    ohigh = {0: beside(high[0])}
    for d in (-1, 1, -2, 2):
        ohigh[d] = beside(high[d])
    for d in (-3, 3):
        olow[d] = beside(low[d])
    olow[4] = beside(low[4])
    ohigh[4] = beside(high[4])
    for d in (1, 2):
        olow[-d] = ahead(olow[1 - d])
        olow[d] = back(olow[d - 1])
    ohigh[-3] = ahead(ohigh[-2])
    ohigh[3] = back(ohigh[2])

    partner_acts = lax.ppermute(train_acts, "core", swap)
    partner_grads = lax.ppermute(train_grads, "core", swap)
    local_ids = train_ids - pair * (2 * SEQ_DEV)
    partner_ids = lax.ppermute(local_ids, "core", swap)
    ids = jnp.stack([local_ids, partner_ids])
    acts = (train_acts, partner_acts)
    grads = (train_grads, partner_grads)

    near = (0, -1, 1, -2, 2, -3, 3)
    set_a = [(low[d], high[d]) for d in near] + [(olow[0], ohigh[0])]
    set_b = [(olow[d], ohigh[d]) for d in (-1, 1, -2, 2)]
    set_c = [(low[4], high[4])] + [(olow[d], ohigh[d]) for d in (-3, 3, 4)]
    na, nb, nc = len(set_a), len(set_b), len(set_c)
    score_shape = (2 * SEQ_DEV, VAL_SEQS)

    def gram_shape(count):
        return (2, tokens, SEQ_DEV * count)

    (low_a,) = call_low(keep_low, acts, [p[0] for p in set_a], [], [gram_shape(na)])
    score, act_b, grad_b, hot_b = call_high(
        lambda *refs: first_high(na, *refs),
        acts,
        grads,
        [p[1] for p in set_a + set_b],
        [ids, low_a],
        [score_shape, gram_shape(nb), gram_shape(nb), (SEQ_DEV * nb, VAL_SEQS)],
    )
    score, low_c = call_low(
        lambda *refs: second_low(nb, *refs),
        acts,
        [p[0] for p in set_b + set_c],
        [ids, score, act_b, grad_b, hot_b],
        [score_shape, gram_shape(nc)],
    )
    (score,) = call_high(
        last_high, acts, grads, [p[1] for p in set_c], [ids, score, low_c], [score_shape]
    )
    del core
    share = VAL_SEQS // sections
    parts = score.reshape(2, SEQ_DEV, sections, share).transpose(2, 0, 1, 3)
    parts = parts.reshape(sections * 2, SEQ_DEV, share)
    taken = lax.all_to_all(parts, ("section", "core"), 0, 0, tiled=True)
    return jnp.sum(taken, axis=0)


def solution(mesh):
    cores = 2
    sections, rest = mesh.devices.shape
    grid = Mesh(mesh.devices.reshape(sections, rest // cores, cores), ("section", "zy", "core"))
    both = ("zy", "core")
    return jax.shard_map(
        on_device,
        mesh=grid,
        in_specs=(
            P("section", both, None),
            P("section", both, None),
            P(both),
            P("section", both, None),
            P("section", both, None),
            P(both),
        ),
        out_specs=P(both, "section"),
        check_vma=False,
    )
```

```python
import jax
import jax.numpy as jnp
from jax import lax
from jax.experimental import pallas as pl
from jax.experimental.pallas import tpu as pltpu
from jax.sharding import Mesh, PartitionSpec as P

SEQ_DEV = 8
VAL_SEQS = 16
LANES = 128
ACT_TILE = 9216
F32 = jnp.float32
HIGHEST = lax.Precision.HIGHEST


def rows_of(blocks, start, size):
    return jnp.concatenate([block[:, pl.ds(start, size)] for block in blocks], axis=0)


def contract(left, piece):
    return lax.dot_general(left, piece, (((1,), (1,)), ((), ())), preferred_element_type=F32)


def train_onehots(ids_ref):
    places = lax.broadcasted_iota(jnp.int32, (2 * SEQ_DEV, ids_ref.shape[1]), 0)
    return [(ids_ref[k : k + 1, :] == places).astype(F32) for k in range(2)]


def val_onehot(blocks):
    width = blocks[0].shape[1]
    numbers = [block[:, width - LANES :].astype(F32)[:, :VAL_SEQS] for block in blocks]
    stacked = jnp.concatenate(numbers, axis=0)
    return (stacked == lax.broadcasted_iota(jnp.int32, stacked.shape, 1).astype(F32)).astype(F32)


def scores_of(onehots, act_grams, grad_grams, val_hot):
    total = None
    for hot, act, grad in zip(onehots, act_grams, grad_grams):
        term = jnp.dot(hot, act * grad, precision=HIGHEST, preferred_element_type=F32)
        total = term if total is None else total + term
    return jnp.dot(total, val_hot, precision=HIGHEST, preferred_element_type=F32)


def act_part(acts, blocks, first, tiles):
    shape = (acts[0].shape[1], SEQ_DEV * len(blocks))

    def step(i, sums):
        at = pl.multiple_of(i * ACT_TILE, LANES)
        piece = rows_of(blocks, at, ACT_TILE)
        of = pl.multiple_of(first * ACT_TILE + i * ACT_TILE, LANES)
        return tuple(s + contract(a[0, :, pl.ds(of, ACT_TILE)], piece) for s, a in zip(sums, acts))

    zero = jnp.zeros(shape, F32)
    return lax.fori_loop(0, tiles, step, (zero, zero))


def grad_part(grads, blocks, start):
    piece = rows_of(blocks, start, grads[0].shape[2])
    return [contract(g[0], piece) for g in grads]


def whole_kernel(*refs):
    acts, grads, ids, blocks, out = refs[:2], refs[2:4], refs[4], refs[5:-1], refs[-1]
    width = acts[0].shape[2]
    act_grams = act_part(acts, blocks, 0, width // ACT_TILE)
    grad_grams = grad_part(grads, blocks, width)
    out[...] = scores_of(train_onehots(ids), act_grams, grad_grams, val_onehot(blocks))


def low_kernel(*refs):
    acts, blocks, out = refs[:2], refs[2:-1], refs[-1]
    sums = act_part(acts, blocks, 0, blocks[0].shape[1] // ACT_TILE)
    out[0] = sums[0]
    out[1] = sums[1]


def high_kernel(*refs):
    acts, grads = refs[:2], refs[2:4]
    ids, low, score = refs[4:7]
    blocks, out = refs[7:-1], refs[-1]
    tiles = (blocks[0].shape[1] - grads[0].shape[2] - LANES) // ACT_TILE
    sums = act_part(acts, blocks, acts[0].shape[2] // ACT_TILE - tiles, tiles)
    act_grams = [sums[k] + low[k] for k in range(2)]
    grad_grams = grad_part(grads, blocks, tiles * ACT_TILE)
    out[...] = score[...] + scores_of(
        train_onehots(ids), act_grams, grad_grams, val_onehot(blocks)
    )


def call(kernel, shape, flops, *operands):
    space = pl.BlockSpec(memory_space=pltpu.VMEM)
    return pl.pallas_call(
        kernel,
        in_specs=[space] * len(operands),
        out_specs=space,
        out_shape=jax.ShapeDtypeStruct(shape, F32),
        compiler_params=pltpu.CompilerParams(vmem_limit_bytes=6 * 1024 * 1024),
        cost_estimate=pl.CostEstimate(flops=flops, bytes_accessed=0, transcendentals=0),
    )(*operands)


def on_device(train_acts, train_grads, train_ids, val_acts, val_grads, val_ids):
    width, tokens = train_acts.shape[2], train_acts.shape[1]
    cut = (width // ACT_TILE * 2 // 3) * ACT_TILE
    pair = lax.axis_index("zy")
    both = ("zy", "core")
    places = lax.axis_size("zy") * 2
    sections = lax.axis_size("section")

    def mover(target):
        pairs = [(i, target(i) % places) for i in range(places)]
        return lambda block: lax.ppermute(block, both, pairs)

    ahead = mover(lambda i: i + 4 if i % 2 == 0 else i - 4)
    back = mover(lambda i: i - 4 if i % 2 == 0 else i + 4)
    beside = mover(lambda i: i ^ 2)
    other_core = mover(lambda i: i ^ 1)

    numbers = jnp.broadcast_to(val_ids.astype(jnp.bfloat16)[:, None], (SEQ_DEV, LANES))
    own, other = {}, {}
    own[0] = jnp.concatenate([val_acts[0], val_grads[0], numbers], axis=1)

    def after(block, *done):
        return lax.optimization_barrier((block, *done))[0]

    def halves(block):
        return block[:, :cut], block[:, cut:]

    other_acts = other_core(train_acts)
    other_grads = other_core(train_grads)
    own[-1] = ahead(own[0])
    own[1] = back(own[0])
    other[0] = beside(own[0])
    own[-2] = ahead(own[-1])
    other[1] = beside(own[1])
    own[2] = back(after(own[1], other[0]))
    own[-3] = ahead(after(own[-2], other_acts, other_grads))
    other[-2] = beside(after(own[-2], other[0]))
    other[2] = back(after(other[1], own[2]))
    own[4] = ahead(own[-3])
    other[-3] = beside(after(own[-3], other[1]))
    own[3] = back(after(own[2], other[2], other[-2]))

    zero_low, zero_high = halves(other[0])
    late_low = [ahead(after(zero_low, own[4]))]
    late_high = [ahead(after(zero_high, late_low[0]))]
    two_low, two_high = halves(other[2])
    late_low.append(back(after(two_low, own[3], other[-3])))
    late_high.append(back(after(two_high, late_low[1])))
    four_low, four_high = halves(own[4])
    late_low.append(beside(after(four_low, other[-2])))
    late_high.append(beside(after(four_high, other[-3])))
    late = list(zip(late_low, late_high))

    acts = (train_acts, other_acts)
    grads = (train_grads, other_grads)
    local_ids = train_ids - pair * (2 * SEQ_DEV)
    ids = jnp.stack([local_ids, other_core(after(local_ids, own[-2]))])

    early = [own[d] for d in (0, -1, 1, -2, 2, -3, 3, 4)] + [other[d] for d in (0, 1, -2, 2, -3)]
    cost = 4 * tokens * 256
    shape = (2 * SEQ_DEV, VAL_SEQS)
    score = call(
        whole_kernel, shape, cost * (width + grads[0].shape[2]), *acts, *grads, ids, *early
    )
    low = call(
        low_kernel,
        (2, tokens, SEQ_DEV * len(late)),
        cost * cut,
        *acts,
        *[block[0] for block in late],
    )
    score = call(
        high_kernel,
        shape,
        cost * (width + grads[0].shape[2] - cut),
        *acts,
        *grads,
        ids,
        low,
        score,
        *[block[1] for block in late],
    )
    share = VAL_SEQS // sections
    parts = score.reshape(2, SEQ_DEV, sections, share).transpose(2, 0, 1, 3)
    parts = parts.reshape(sections * 2, SEQ_DEV, share)
    taken = lax.all_to_all(parts, ("section", "core"), 0, 0, tiled=True)
    return jnp.sum(taken, axis=0)


def solution(mesh):
    cores = 2
    sections, rest = mesh.devices.shape
    grid = Mesh(mesh.devices.reshape(sections, rest // cores, cores), ("section", "zy", "core"))
    both = ("zy", "core")
    return jax.shard_map(
        on_device,
        mesh=grid,
        in_specs=(
            P("section", both, None),
            P("section", both, None),
            P(both),
            P("section", both, None),
            P("section", both, None),
            P(both),
        ),
        out_specs=P(both, "section"),
        check_vma=False,
    )
```

```python
import jax
import jax.numpy as jnp
from jax import lax
from jax.experimental import pallas as pl
from jax.experimental.pallas import tpu as pltpu
from jax.sharding import Mesh, PartitionSpec as P

SEQ_DEV = 8
VAL_SEQS = 16
LANES = 128
ACT_TILE = 4608
F32 = jnp.float32
HIGHEST = lax.Precision.HIGHEST


def rows_of(blocks, start, size):
    return jnp.concatenate([block[:, pl.ds(start, size)] for block in blocks], axis=0)


def contract(left, piece):
    return lax.dot_general(left, piece, (((1,), (1,)), ((), ())), preferred_element_type=F32)


def train_onehots(ids_ref):
    places = lax.broadcasted_iota(jnp.int32, (2 * SEQ_DEV, ids_ref.shape[1]), 0)
    return [(ids_ref[k : k + 1, :] == places).astype(F32) for k in range(2)]


def val_onehot(blocks):
    width = blocks[0].shape[1]
    numbers = [block[:, width - LANES :].astype(F32)[:, :VAL_SEQS] for block in blocks]
    stacked = jnp.concatenate(numbers, axis=0)
    return (stacked == lax.broadcasted_iota(jnp.int32, stacked.shape, 1).astype(F32)).astype(F32)


def scores_of(onehots, act_grams, grad_grams, val_hot):
    total = None
    for hot, act, grad in zip(onehots, act_grams, grad_grams):
        term = jnp.dot(hot, act * grad, precision=HIGHEST, preferred_element_type=F32)
        total = term if total is None else total + term
    return jnp.dot(total, val_hot, precision=HIGHEST, preferred_element_type=F32)


def fetch_acts(acts, buffer, sem):
    tiles = [
        [
            pltpu.make_async_copy(
                act.at[0, :, pl.ds(i * ACT_TILE, ACT_TILE)], buffer.at[k, i], sem.at[k, i]
            )
            for k, act in enumerate(acts)
        ]
        for i in range(buffer.shape[1])
    ]
    for tile in tiles:
        for copy in tile:
            copy.start()
    return tiles


def fetch_grads(grads, buffer, sem):
    copies = [
        pltpu.make_async_copy(grad.at[0], buffer.at[k], sem.at[k]) for k, grad in enumerate(grads)
    ]
    for copy in copies:
        copy.start()
    return copies


def act_part(tiles, buffer, blocks):
    sums = [0.0, 0.0]
    for i, tile in enumerate(tiles):
        piece = rows_of(blocks, i * ACT_TILE, ACT_TILE)
        for k, copy in enumerate(tile):
            copy.wait()
            sums[k] = sums[k] + contract(buffer[k, i], piece)
    return sums


def grad_part(copies, buffer, blocks, start):
    piece = rows_of(blocks, start, buffer.shape[2])
    sums = []
    for k, copy in enumerate(copies):
        copy.wait()
        sums.append(contract(buffer[k], piece))
    return sums


def score_part(acts, grads, ids, blocks, act_buf, grad_buf, act_sem, grad_sem):
    tiles = fetch_acts(acts, act_buf, act_sem)
    copies = fetch_grads(grads, grad_buf, grad_sem)

    def finish():
        act_grams = act_part(tiles, act_buf, blocks)
        grad_grams = grad_part(copies, grad_buf, blocks, acts[0].shape[2])
        return scores_of(train_onehots(ids), act_grams, grad_grams, val_onehot(blocks))

    return finish


def early_kernel(*refs):
    acts, grads, ids = refs[:2], refs[2:4], refs[4]
    held, out = refs[5:-7], refs[-7]
    act_buf, grad_buf, val_buf, act_sem, grad_sem, val_sem = refs[-6:]
    blocks = [val_buf.at[i] for i in range(len(held))]
    moves = [
        pltpu.make_async_copy(source, block, val_sem.at[i])
        for i, (source, block) in enumerate(zip(held, blocks))
    ]
    for move in moves:
        move.start()
    finish = score_part(acts, grads, ids, blocks, act_buf, grad_buf, act_sem, grad_sem)
    for move in moves:
        move.wait()
    out[...] = finish()


def late_kernel(*refs):
    acts, grads, ids, score = refs[:2], refs[2:4], refs[4], refs[5]
    blocks, out = refs[6:-5], refs[-5]
    out[...] = score[...] + score_part(acts, grads, ids, blocks, *refs[-4:])()


def call(kernel, scratch, flops, mebibytes, operands, near):
    return pl.pallas_call(
        kernel,
        in_specs=[
            pl.BlockSpec(memory_space=pltpu.VMEM if i in near else pltpu.HBM)
            for i in range(len(operands))
        ],
        out_specs=pl.BlockSpec(memory_space=pltpu.VMEM),
        out_shape=jax.ShapeDtypeStruct((2 * SEQ_DEV, VAL_SEQS), F32),
        scratch_shapes=scratch,
        compiler_params=pltpu.CompilerParams(vmem_limit_bytes=mebibytes * 1024 * 1024),
        cost_estimate=pl.CostEstimate(flops=flops, bytes_accessed=0, transcendentals=0),
    )(*operands)


def on_device(train_acts, train_grads, train_ids, val_acts, val_grads, val_ids):
    width, tokens = train_acts.shape[2], train_acts.shape[1]
    pair = lax.axis_index("zy")
    both = ("zy", "core")
    places = lax.axis_size("zy") * 2
    sections = lax.axis_size("section")

    def mover(target):
        pairs = [(i, target(i) % places) for i in range(places)]
        return lambda block: lax.ppermute(block, both, pairs)

    ahead = mover(lambda i: i + 4 if i % 2 == 0 else i - 4)
    back = mover(lambda i: i - 4 if i % 2 == 0 else i + 4)
    beside = mover(lambda i: i ^ 2)
    other_core = mover(lambda i: i ^ 1)

    numbers = jnp.broadcast_to(val_ids.astype(jnp.bfloat16)[:, None], (SEQ_DEV, LANES))
    own, other = {}, {}
    own[0] = jnp.concatenate([val_acts[0], val_grads[0], numbers], axis=1)

    def after(block, *done):
        return lax.optimization_barrier((block, *done))[0]

    other_ids = other_core(train_ids)
    other_grads = other_core(train_grads)
    other_acts = other_core(train_acts)
    own[-1] = ahead(own[0])
    other[0] = beside(own[0])
    own[1] = back(after(own[0], other_ids, other_grads))
    own[-2] = ahead(own[-1])
    other[1] = beside(own[1])
    own[2] = back(after(own[1], other[0]))
    own[-3] = ahead(after(own[-2], other_acts))
    other[-2] = beside(after(own[-2], other[0]))
    other[2] = back(after(other[1], own[2]))
    own[4] = ahead(own[-3])
    other[-3] = beside(after(own[-3], other[1]))
    own[3] = back(after(own[2], other[2], other[-2]))

    late = [
        ahead(after(other[0], own[4])),
        back(after(other[2], own[3], other[-3])),
        beside(after(own[4], other[-2])),
    ]

    ids = jnp.stack([train_ids, other_ids]) - pair * (2 * SEQ_DEV)
    acts = (train_acts, other_acts)
    grads = (train_grads, other_grads)
    early = [own[d] for d in (0, -1, 1, -2, 2, -3, 3, 4)] + [other[d] for d in (0, 1, -2, 2, -3)]
    grad_width = train_grads.shape[2]
    bf16, copies = jnp.bfloat16, pltpu.SemaphoreType.DMA

    tiles = width // ACT_TILE
    buffers = [
        pltpu.VMEM((2, tiles, tokens, ACT_TILE), bf16),
        pltpu.VMEM((2, tokens, grad_width), bf16),
    ]
    marks = [copies((2, tiles)), copies((2,))]
    held = pltpu.VMEM((len(early), *own[0].shape), bf16)
    cost = 4 * tokens * 256 * (width + grad_width)
    score = call(
        early_kernel,
        [*buffers, held, *marks, copies((len(early),))],
        cost,
        56,
        [*acts, *grads, ids, *early],
        [4],
    )
    score = call(
        late_kernel,
        [*buffers, *marks],
        cost,
        40,
        [*acts, *grads, ids, score, *late],
        [4, 5, 6, 7, 8],
    )
    share = VAL_SEQS // sections
    parts = score.reshape(2, SEQ_DEV, sections, share).transpose(2, 0, 1, 3)
    parts = parts.reshape(sections * 2, SEQ_DEV, share)
    taken = lax.all_to_all(parts, ("section", "core"), 0, 0, tiled=True)
    return jnp.sum(taken, axis=0)


def solution(mesh):
    cores = 2
    sections, rest = mesh.devices.shape
    grid = Mesh(mesh.devices.reshape(sections, rest // cores, cores), ("section", "zy", "core"))
    both = ("zy", "core")
    return jax.shard_map(
        on_device,
        mesh=grid,
        in_specs=(
            P("section", both, None),
            P("section", both, None),
            P(both),
            P("section", both, None),
            P("section", both, None),
            P(both),
        ),
        out_specs=P(both, "section"),
        check_vma=False,
    )
```

```python
import jax
import jax.numpy as jnp
from jax import lax
from jax.experimental import pallas as pl
from jax.experimental.pallas import tpu as pltpu
from jax.sharding import Mesh, PartitionSpec as P

SEQ_DEV = 8
VAL_SEQS = 16
LANES = 128
ACT_TILE = 9216
VMEM_MIB = 6
F32 = jnp.float32
HIGHEST = lax.Precision.HIGHEST


def rows_of(blocks, start, size):
    return jnp.concatenate([block[:, pl.ds(start, size)] for block in blocks], axis=0)


def contract(left, piece):
    return lax.dot_general(left, piece, (((1,), (1,)), ((), ())), preferred_element_type=F32)


def train_onehots(ids_ref):
    places = lax.broadcasted_iota(jnp.int32, (2 * SEQ_DEV, ids_ref.shape[1]), 0)
    return [(ids_ref[k : k + 1, :] == places).astype(F32) for k in range(2)]


def val_onehot(blocks):
    width = blocks[0].shape[1]
    numbers = [block[:, width - LANES :].astype(F32)[:, :VAL_SEQS] for block in blocks]
    stacked = jnp.concatenate(numbers, axis=0)
    return (stacked == lax.broadcasted_iota(jnp.int32, stacked.shape, 1).astype(F32)).astype(F32)


def scores_of(onehots, act_grams, grad_grams, val_hot):
    total = None
    for hot, act, grad in zip(onehots, act_grams, grad_grams):
        term = jnp.dot(hot, act * grad, precision=HIGHEST, preferred_element_type=F32)
        total = term if total is None else total + term
    return jnp.dot(total, val_hot, precision=HIGHEST, preferred_element_type=F32)


def act_part(act, blocks):
    total = 0.0
    for start in range(0, act.shape[2], ACT_TILE):
        piece = rows_of(blocks, start, ACT_TILE)
        total = total + contract(act[0, :, start : start + ACT_TILE], piece)
    return total


def grad_part(grads, blocks, start):
    piece = rows_of(blocks, start, grads[0].shape[2])
    return [contract(g[0], piece) for g in grads]


def early_kernel(*refs):
    source, own, grads, ids = refs[0], refs[1], refs[2:4], refs[4]
    blocks, out, target, sem = refs[5:-3], refs[-3], refs[-2], refs[-1]
    copy = pltpu.make_async_copy(source, target, sem)
    copy.start()
    grad_grams = grad_part(grads, blocks, own.shape[2])
    own_gram = act_part(own, blocks)
    copy.wait()
    act_grams = [own_gram, act_part(target, blocks)]
    out[...] = scores_of(train_onehots(ids), act_grams, grad_grams, val_onehot(blocks))


def late_kernel(*refs):
    acts, grads, ids, score = refs[:2], refs[2:4], refs[4], refs[5]
    blocks, out = refs[6:-1], refs[-1]
    act_grams = [act_part(act, blocks) for act in acts]
    grad_grams = grad_part(grads, blocks, acts[0].shape[2])
    out[...] = score[...] + scores_of(
        train_onehots(ids), act_grams, grad_grams, val_onehot(blocks)
    )


def call(kernel, spaces, shapes, operands, scratch=(), flops=0):
    return pl.pallas_call(
        kernel,
        in_specs=[pl.BlockSpec(memory_space=space) for space in spaces],
        out_specs=[pl.BlockSpec(memory_space=pltpu.VMEM)] * len(shapes),
        out_shape=[jax.ShapeDtypeStruct(shape, dtype) for shape, dtype in shapes],
        scratch_shapes=list(scratch),
        compiler_params=pltpu.CompilerParams(vmem_limit_bytes=VMEM_MIB * 1024 * 1024),
        cost_estimate=pl.CostEstimate(flops=flops, bytes_accessed=0, transcendentals=0),
    )(*operands)


def on_device(train_acts, train_grads, train_ids, val_acts, val_grads, val_ids):
    width, tokens = train_acts.shape[2], train_acts.shape[1]
    pair = lax.axis_index("zy")
    both = ("zy", "core")
    places = lax.axis_size("zy") * 2
    sections = lax.axis_size("section")

    def mover(target):
        pairs = [(i, target(i) % places) for i in range(places)]
        return lambda block: lax.ppermute(block, both, pairs)

    ahead = mover(lambda i: i + 4 if i % 2 == 0 else i - 4)
    back = mover(lambda i: i - 4 if i % 2 == 0 else i + 4)
    beside = mover(lambda i: i ^ 2)
    other_core = mover(lambda i: i ^ 1)

    numbers = jnp.broadcast_to(val_ids.astype(jnp.bfloat16)[:, None], (SEQ_DEV, LANES))
    own, other = {}, {}
    own[0] = jnp.concatenate([val_acts[0], val_grads[0], numbers], axis=1)

    def after(block, *done):
        return lax.optimization_barrier((block, *done))[0]

    other_grads = other_core(train_grads)
    other_ids = other_core(after(train_ids, other_grads))
    other_acts = other_core(after(train_acts, other_ids))
    own[-1] = ahead(own[0])
    other[0] = beside(own[0])
    own[1] = back(after(own[0], other_ids))
    own[-2] = ahead(own[-1])
    other[1] = beside(own[1])
    own[2] = back(after(own[1], other[0]))
    own[-3] = ahead(own[-2])
    other[-2] = beside(after(own[-2], other[0]))
    other[2] = back(after(other[1], own[2]))
    own[4] = ahead(own[-3])
    other[-3] = beside(after(own[-3], other[1]))
    own[3] = back(after(own[2], other[2], other[-2]))
    late = [
        ahead(after(other[0], own[4])),
        back(after(other[2], own[3], other[-3])),
        beside(after(own[4], other[-2])),
    ]

    ids = jnp.stack([train_ids, other_ids]) - pair * (2 * SEQ_DEV)
    early = [own[d] for d in (0, -1, 1, -2, 2, -3, 3, 4)] + [other[d] for d in (0, 1, -2, 2, -3)]
    vmem = pltpu.VMEM
    cost = 4 * tokens * 256 * (width + train_grads.shape[2])
    near = [train_acts, train_grads, other_grads, ids, *early]
    score_shape = ((2 * SEQ_DEV, VAL_SEQS), F32)
    score, fetched = call(
        early_kernel,
        [pltpu.HBM] + [vmem] * len(near),
        [score_shape, (other_acts.shape, other_acts.dtype)],
        [other_acts, *near],
        [pltpu.SemaphoreType.DMA],
        cost,
    )
    operands = [train_acts, fetched, train_grads, other_grads, ids, score, *late]
    (score,) = call(late_kernel, [vmem] * len(operands), [score_shape], operands, (), cost)
    share = VAL_SEQS // sections
    parts = score.reshape(2, SEQ_DEV, sections, share).transpose(2, 0, 1, 3)
    parts = parts.reshape(sections * 2, SEQ_DEV, share)
    taken = lax.all_to_all(parts, ("section", "core"), 0, 0, tiled=True)
    return jnp.sum(taken, axis=0)


def solution(mesh):
    cores = 2
    sections, rest = mesh.devices.shape
    grid = Mesh(mesh.devices.reshape(sections, rest // cores, cores), ("section", "zy", "core"))
    both = ("zy", "core")
    return jax.shard_map(
        on_device,
        mesh=grid,
        in_specs=(
            P("section", both, None),
            P("section", both, None),
            P(both),
            P("section", both, None),
            P("section", both, None),
            P(both),
        ),
        out_specs=P(both, "section"),
        check_vma=False,
    )
```

```python
import functools

import jax
import jax.numpy as jnp
from jax import lax
from jax.experimental import pallas as pl
from jax.experimental.pallas import tpu as pltpu
from jax.sharding import Mesh, PartitionSpec as P

SEQ_DEV = 8
VAL_SEQS = 16
LANES = 128
ACT_TILES = 2
EARLY_MIB = 30
LATE_MIB = 8
MIRROR = (0, 2, 1, 4, 3, 6, 5, 7, 8, 10, 9, 11, 12)
F32 = jnp.float32
HIGHEST = lax.Precision.HIGHEST


def contract(left, piece):
    return lax.dot_general(left, piece, (((1,), (1,)), ((), ())), preferred_element_type=F32)


def grams(train, blocks, act_width, grad_width):
    tile = act_width // ACT_TILES
    starts = [(i * tile, tile) for i in range(ACT_TILES)] + [(act_width, grad_width)]
    parts = []
    for start, size in starts:
        piece = jnp.concatenate([block[:, start : start + size] for block in blocks], axis=0)
        parts.append(contract(train[:, start : start + size], piece))
    return sum(parts[1:-1], parts[0]), parts[-1]


def val_onehot(blocks):
    width = blocks[0].shape[1]
    numbers = [block[:, width - LANES :].astype(F32)[:, :VAL_SEQS] for block in blocks]
    stacked = jnp.concatenate(numbers, axis=0)
    return (stacked == lax.broadcasted_iota(jnp.int32, stacked.shape, 1).astype(F32)).astype(F32)


def early_kernel(act_width, grad_width, *refs):
    core, sources = refs[0][0], (refs[1:3], refs[3:5])
    blocks, (kept, sent, hot, own, partner, sems) = refs[5:-6], refs[-6:]
    copies = []
    for k, (pair, target) in enumerate(zip(sources, (own, partner))):
        begin = 0
        for j, (source, size) in enumerate(zip(pair, (act_width, grad_width))):
            held = source.at[0, :, pl.ds(pl.multiple_of(core * size, LANES), size)]
            copies.append(
                pltpu.make_async_copy(held, target.at[:, begin : begin + size], sems.at[k, j])
            )
            begin += size
    for copy in copies:
        copy.start()
    hot[...] = val_onehot(blocks)
    copies[0].wait()
    copies[1].wait()
    kept[0], kept[1] = grams(own, blocks, act_width, grad_width)
    copies[2].wait()
    copies[3].wait()
    mirrored = [blocks[i] for i in MIRROR]
    sent[0], sent[1] = grams(partner, mirrored, act_width, grad_width)


def late_kernel(act_width, grad_width, *refs):
    own, partner = refs[:2]
    blocks, (kept, sent, hot) = refs[2:-3], refs[-3:]
    kept[0], kept[1] = grams(own, blocks, act_width, grad_width)
    sent[0], sent[1] = grams(partner, blocks, act_width, grad_width)
    hot[...] = val_onehot(blocks)


def score_kernel(ids, *refs):
    early, late, out = refs[:3], refs[3:6], refs[-1]
    odd = 4 * SEQ_DEV
    by_val = 0.0
    for (kept, _, hot), (_, came, _), same in (
        (early, early, True),
        (late, late, True),
        (early, late, False),
        (late, early, False),
    ):
        width, reach = kept.shape[2], came.shape[2]
        here = slice(0, width - odd) if same else slice(width - odd, width)
        there = slice(0, reach - odd) if same else slice(reach - odd, reach)
        sums = [kept[k][:, here] + came[k][:, there] for k in range(2)]
        by_val = by_val + jnp.dot(
            sums[0] * sums[1], hot[here, :], precision=HIGHEST, preferred_element_type=F32
        )
    places = lax.broadcasted_iota(jnp.int32, (SEQ_DEV, ids.shape[1]), 0)
    onehot = (ids[...] == places).astype(F32)
    out[...] = jnp.dot(onehot, by_val, precision=HIGHEST, preferred_element_type=F32)


def call(kernel, spaces, shapes, operands, mebibytes, scratch=(), flops=0):
    return pl.pallas_call(
        kernel,
        in_specs=[pl.BlockSpec(memory_space=space) for space in spaces],
        out_specs=[pl.BlockSpec(memory_space=pltpu.VMEM)] * len(shapes),
        out_shape=[jax.ShapeDtypeStruct(shape, dtype) for shape, dtype in shapes],
        scratch_shapes=list(scratch),
        compiler_params=pltpu.CompilerParams(vmem_limit_bytes=mebibytes * 1024 * 1024),
        cost_estimate=pl.CostEstimate(flops=flops, bytes_accessed=0, transcendentals=0),
    )(*operands)


def after(block, *done):
    return lax.optimization_barrier((block, *done))[0]


def on_device(train_acts, train_grads, train_ids, val_acts, val_grads, val_ids):
    tokens = train_acts.shape[1]
    act_width, grad_width = train_acts.shape[2] // 2, train_grads.shape[2] // 2
    both = ("zy", "core")
    places = lax.axis_size("zy") * 2
    sections = lax.axis_size("section")
    core = lax.axis_index("core")

    def mover(target):
        pairs = [(i, target(i) % places) for i in range(places)]
        return lambda block: lax.ppermute(block, both, pairs)

    ahead = mover(lambda i: i + 4 if i % 2 == 0 else i - 4)
    back = mover(lambda i: i - 4 if i % 2 == 0 else i + 4)
    beside = mover(lambda i: i ^ 2)
    other_core = mover(lambda i: i ^ 1)

    def columns(acts, grads, which):
        return [
            lax.dynamic_slice_in_dim(acts[0], which * act_width, act_width, 1),
            lax.dynamic_slice_in_dim(grads[0], which * grad_width, grad_width, 1),
        ]

    numbers = jnp.broadcast_to(val_ids.astype(jnp.bfloat16)[:, None], (SEQ_DEV, LANES))
    mine = jnp.concatenate([*columns(val_acts, val_grads, core), numbers], axis=1)
    theirs = jnp.concatenate([*columns(val_acts, val_grads, 1 - core), numbers], axis=1)
    own, other = {}, {}
    came = other_core(theirs)
    first = core == 0
    own[0] = jnp.concatenate(
        [jnp.where(first, mine, came), jnp.where(first, came, mine)], axis=0
    )

    other_grads = other_core(after(train_grads, own[0]))
    other_acts = other_core(after(train_acts, own[0]))
    own[-1] = ahead(own[0])
    other[0] = beside(own[0])
    own[1] = back(own[0])
    own[-2] = ahead(own[-1])
    other[1] = beside(own[1])
    own[2] = back(after(own[1], other[0]))
    own[-3] = ahead(own[-2])
    other[-2] = beside(after(own[-2], other[0]))
    other[2] = back(after(other[1], own[2]))
    own[4] = ahead(own[-3])
    other[-3] = beside(after(own[-3], other[1]))
    own[3] = back(after(own[2], other[2], other[-2]))
    late = [
        beside(after(own[4], other[-2])),
        ahead(after(other[0], own[4])),
        back(after(other[2], own[3], other[-3])),
    ]
    early = [own[d] for d in (0, -1, 1, -2, 2, -3, 3, 4)] + [other[d] for d in (0, -2, 2, 1, -3)]

    vmem, hbm = pltpu.VMEM, pltpu.HBM
    cost = 4 * tokens * 256 * (act_width + grad_width)
    rows_shape = ((tokens, act_width + grad_width), train_acts.dtype)

    def outputs(blocks):
        count = len(blocks) * blocks[0].shape[0]
        return [((2, tokens, count), F32), ((2, tokens, count), F32), ((count, VAL_SEQS), F32)]

    kept, sent, hot, rows, partner = call(
        functools.partial(early_kernel, act_width, grad_width),
        [pltpu.SMEM] + [hbm] * 4 + [vmem] * len(early),
        outputs(early) + [rows_shape] * 2,
        [core.reshape(1), train_acts, train_grads, other_acts, other_grads, *early],
        EARLY_MIB,
        [pltpu.SemaphoreType.DMA((2, 2))],
        cost,
    )
    late_kept, late_sent, late_hot = call(
        functools.partial(late_kernel, act_width, grad_width),
        [vmem] * (2 + len(late)),
        outputs(late),
        [rows, partner, *late],
        LATE_MIB,
        (),
        cost,
    )
    local_ids = train_ids - (lax.axis_index("zy") * 2 + core) * SEQ_DEV
    operands = [local_ids[None, :], kept, other_core(sent), hot]
    operands += [late_kept, other_core(late_sent), late_hot]
    (score,) = call(
        score_kernel, [vmem] * len(operands), [((SEQ_DEV, VAL_SEQS), F32)], operands, LATE_MIB
    )
    share = VAL_SEQS // sections
    parts = score.reshape(SEQ_DEV, sections, share).transpose(1, 0, 2)
    return jnp.sum(lax.all_to_all(parts, "section", 0, 0, tiled=True), axis=0)


def solution(mesh):
    cores = 2
    sections, rest = mesh.devices.shape
    grid = Mesh(mesh.devices.reshape(sections, rest // cores, cores), ("section", "zy", "core"))
    both = ("zy", "core")
    return jax.shard_map(
        on_device,
        mesh=grid,
        in_specs=(
            P("section", both, None),
            P("section", both, None),
            P(both),
            P("section", both, None),
            P("section", both, None),
            P(both),
        ),
        out_specs=P(both, "section"),
        check_vma=False,
    )
```

```python
import functools

import jax
import jax.numpy as jnp
from jax import lax
from jax.experimental import pallas as pl
from jax.experimental.pallas import tpu as pltpu
from jax.sharding import Mesh, PartitionSpec as P

SEQ_DEV = 8
VAL_SEQS = 16
LANES = 128
ACT_TILES = 2
FETCH_MIB = 22
LATE_MIB = 8
MIRROR = (0, 2, 1, 4, 3, 6, 5, 7, 8, 10, 9, 14, 15, 13, 11, 12)
F32 = jnp.float32
HIGHEST = lax.Precision.HIGHEST


def contract(left, piece):
    return lax.dot_general(left, piece, (((1,), (1,)), ((), ())), preferred_element_type=F32)


def grams(train, blocks, act_width, grad_width):
    tile = act_width // ACT_TILES
    starts = [(i * tile, tile) for i in range(ACT_TILES)] + [(act_width, grad_width)]
    parts = []
    for start, size in starts:
        piece = jnp.concatenate([block[:, start : start + size] for block in blocks], axis=0)
        parts.append(contract(train[:, start : start + size], piece))
    return sum(parts[1:-1], parts[0]), parts[-1]


def val_onehot(blocks):
    width = blocks[0].shape[1]
    numbers = [block[:, width - LANES :].astype(F32)[:, :VAL_SEQS] for block in blocks]
    stacked = jnp.concatenate(numbers, axis=0)
    return (stacked == lax.broadcasted_iota(jnp.int32, stacked.shape, 1).astype(F32)).astype(F32)


def fetch_kernel(act_width, grad_width, *refs):
    core, sources = refs[0][0], (refs[1:3], refs[3:5])
    blocks, (own, partner, stack, sems, val_sems) = refs[5:-5], refs[-5:]
    copies = [
        pltpu.make_async_copy(block, stack.at[i], val_sems.at[i]) for i, block in enumerate(blocks)
    ]
    for k, (pair, target) in enumerate(zip(sources, (own, partner))):
        begin = 0
        for j, (source, size) in enumerate(zip(pair, (act_width, grad_width))):
            held = source.at[0, :, pl.ds(pl.multiple_of(core * size, LANES), size)]
            copies.append(
                pltpu.make_async_copy(held, target.at[:, begin : begin + size], sems.at[k, j])
            )
            begin += size
    for copy in copies:
        copy.start()
    for copy in copies:
        copy.wait()


def gram_kernel(act_width, grad_width, rows, partner, stack, *refs):
    late, (kept, sent, hot) = refs[:-3], refs[-3:]
    blocks = [stack.at[i] for i in range(stack.shape[0])] + list(late)
    mirrored = [blocks[i] for i in MIRROR]
    sent[0], sent[1] = grams(partner, mirrored, act_width, grad_width)
    kept[0], kept[1] = grams(rows, blocks, act_width, grad_width)
    hot[...] = val_onehot(blocks)


def score_kernel(ids, kept, came, hot, out):
    product = (kept[0] + came[0]) * (kept[1] + came[1])
    by_val = jnp.dot(product, hot[...], precision=HIGHEST, preferred_element_type=F32)
    places = lax.broadcasted_iota(jnp.int32, (SEQ_DEV, ids.shape[1]), 0)
    onehot = (ids[...] == places).astype(F32)
    out[...] = jnp.dot(onehot, by_val, precision=HIGHEST, preferred_element_type=F32)


def call(kernel, spaces, shapes, operands, mebibytes, scratch=(), flops=0):
    return pl.pallas_call(
        kernel,
        in_specs=[pl.BlockSpec(memory_space=space) for space in spaces],
        out_specs=[pl.BlockSpec(memory_space=pltpu.VMEM)] * len(shapes),
        out_shape=[jax.ShapeDtypeStruct(shape, dtype) for shape, dtype in shapes],
        scratch_shapes=list(scratch),
        compiler_params=pltpu.CompilerParams(vmem_limit_bytes=mebibytes * 1024 * 1024),
        cost_estimate=pl.CostEstimate(flops=flops, bytes_accessed=0, transcendentals=0),
    )(*operands)


def after(block, *done):
    return lax.optimization_barrier((block, *done))[0]


def on_device(train_acts, train_grads, train_ids, val_acts, val_grads, val_ids):
    tokens = train_acts.shape[1]
    act_width, grad_width = train_acts.shape[2] // 2, train_grads.shape[2] // 2
    both = ("zy", "core")
    places = lax.axis_size("zy") * 2
    sections = lax.axis_size("section")
    core = lax.axis_index("core")

    def mover(target):
        pairs = [(i, target(i) % places) for i in range(places)]
        return lambda block: lax.ppermute(block, both, pairs)

    ahead = mover(lambda i: i + 4 if i % 2 == 0 else i - 4)
    back = mover(lambda i: i - 4 if i % 2 == 0 else i + 4)
    beside = mover(lambda i: i ^ 2)
    other_core = mover(lambda i: i ^ 1)

    def columns(acts, grads, which):
        return [
            lax.dynamic_slice_in_dim(acts[0], which * act_width, act_width, 1),
            lax.dynamic_slice_in_dim(grads[0], which * grad_width, grad_width, 1),
        ]

    numbers = jnp.broadcast_to(val_ids.astype(jnp.bfloat16)[:, None], (SEQ_DEV, LANES))
    mine = jnp.concatenate([*columns(val_acts, val_grads, core), numbers], axis=1)
    theirs = jnp.concatenate([*columns(val_acts, val_grads, 1 - core), numbers], axis=1)
    own, other = {}, {}
    came = other_core(theirs)
    first = core == 0
    own[0] = jnp.concatenate(
        [jnp.where(first, mine, came), jnp.where(first, came, mine)], axis=0
    )

    other_grads = other_core(after(train_grads, own[0]))
    other_acts = other_core(after(train_acts, own[0]))
    own[-1] = ahead(own[0])
    other[0] = beside(own[0])
    own[1] = back(own[0])
    own[-2] = ahead(own[-1])
    other[1] = beside(own[1])
    own[2] = back(after(own[1], other[0]))
    own[-3] = ahead(own[-2])
    other[-2] = beside(after(own[-2], other[0]))
    other[2] = back(after(other[1], own[2]))
    own[4] = ahead(own[-3])
    other[-3] = beside(after(own[-3], other[1]))
    own[3] = back(after(own[2], other[2], other[-2]))
    late = [
        beside(after(own[4], other[-2])),
        ahead(after(other[0], own[4])),
        back(after(other[2], own[3], other[-3])),
    ]
    early = [own[d] for d in (0, -1, 1, -2, 2, -3, 3, 4)] + [other[d] for d in (0, -2, 2, 1, -3)]

    vmem, hbm = pltpu.VMEM, pltpu.HBM
    cost = 4 * tokens * 256 * (act_width + grad_width)
    rows_shape = ((tokens, act_width + grad_width), train_acts.dtype)

    widths = (act_width, grad_width)
    stack_shape = ((len(early), *own[0].shape), own[0].dtype)
    gram_shape = ((2, tokens, len(MIRROR) * own[0].shape[0]), F32)
    hot_shape = ((len(MIRROR) * own[0].shape[0], VAL_SEQS), F32)
    rows, partner, stack = call(
        functools.partial(fetch_kernel, *widths),
        [pltpu.SMEM] + [hbm] * (4 + len(early)),
        [rows_shape, rows_shape, stack_shape],
        [core.reshape(1), train_acts, train_grads, other_acts, other_grads, *early],
        FETCH_MIB,
        [pltpu.SemaphoreType.DMA((2, 2)), pltpu.SemaphoreType.DMA((len(early),))],
    )
    kept, sent, hot = call(
        functools.partial(gram_kernel, *widths),
        [vmem] * (3 + len(late)),
        [gram_shape, gram_shape, hot_shape],
        [rows, partner, stack, *late],
        LATE_MIB,
        (),
        cost,
    )
    local_ids = train_ids - (lax.axis_index("zy") * 2 + core) * SEQ_DEV
    operands = [local_ids[None, :], kept, other_core(sent), hot]
    (score,) = call(
        score_kernel, [vmem] * len(operands), [((SEQ_DEV, VAL_SEQS), F32)], operands, LATE_MIB
    )
    share = VAL_SEQS // sections
    parts = score.reshape(SEQ_DEV, sections, share).transpose(1, 0, 2)
    return jnp.sum(lax.all_to_all(parts, "section", 0, 0, tiled=True), axis=0)


def solution(mesh):
    cores = 2
    sections, rest = mesh.devices.shape
    grid = Mesh(mesh.devices.reshape(sections, rest // cores, cores), ("section", "zy", "core"))
    both = ("zy", "core")
    return jax.shard_map(
        on_device,
        mesh=grid,
        in_specs=(
            P("section", both, None),
            P("section", both, None),
            P(both),
            P("section", both, None),
            P("section", both, None),
            P(both),
        ),
        out_specs=P(both, "section"),
        check_vma=False,
    )
```

```python
import functools

import jax
import jax.numpy as jnp
from jax import lax
from jax.experimental import pallas as pl
from jax.experimental.pallas import tpu as pltpu
from jax.sharding import Mesh, PartitionSpec as P

SEQ_DEV = 8
VAL_SEQS = 16
LANES = 128
ACT_TILES = 2
FETCH_MIB = 22
FIRST_MIB = 52
LATE_MIB = 8
MIRROR = (0, 2, 1, 4, 3, 6, 5, 7, 8, 10, 9, 14, 15, 13, 11, 12)
F32 = jnp.float32
HIGHEST = lax.Precision.HIGHEST


def contract(left, piece):
    return lax.dot_general(left, piece, (((1,), (1,)), ((), ())), preferred_element_type=F32)


def grams(train, blocks, act_width, grad_width):
    tile = act_width // ACT_TILES
    starts = [(i * tile, tile) for i in range(ACT_TILES)] + [(act_width, grad_width)]
    parts = []
    for start, size in starts:
        piece = jnp.concatenate([block[:, start : start + size] for block in blocks], axis=0)
        parts.append(contract(train[:, start : start + size], piece))
    return sum(parts[1:-1], parts[0]), parts[-1]


def val_onehot(blocks):
    width = blocks[0].shape[1]
    numbers = [block[:, width - LANES :].astype(F32)[:, :VAL_SEQS] for block in blocks]
    stacked = jnp.concatenate(numbers, axis=0)
    return (stacked == lax.broadcasted_iota(jnp.int32, stacked.shape, 1).astype(F32)).astype(F32)


def fetch_kernel(act_width, grad_width, *refs):
    core, sources = refs[0][0], (refs[1:3], refs[3:5])
    blocks, (own, partner, stack, sems, val_sems) = refs[5:-5], refs[-5:]
    copies = [
        pltpu.make_async_copy(block, stack.at[i], val_sems.at[i]) for i, block in enumerate(blocks)
    ]
    for k, (pair, target) in enumerate(zip(sources, (own, partner))):
        begin = 0
        for j, (source, size) in enumerate(zip(pair, (act_width, grad_width))):
            held = source.at[0, :, pl.ds(pl.multiple_of(core * size, LANES), size)]
            copies.append(
                pltpu.make_async_copy(held, target.at[:, begin : begin + size], sems.at[k, j])
            )
            begin += size
    for copy in copies:
        copy.start()
    for copy in copies:
        copy.wait()


def first_kernel(turn, act_width, grad_width, core_ref, acts, grads, block, before, out, rows, sems):
    core = core_ref[0]

    @pl.when(core == turn)
    def _():
        begin, copies = 0, []
        for j, (source, size) in enumerate(((acts, act_width), (grads, grad_width))):
            held = source.at[0, :, pl.ds(pl.multiple_of(core * size, LANES), size)]
            copies.append(
                pltpu.make_async_copy(held, rows.at[:, begin : begin + size], sems.at[j])
            )
            begin += size
        for copy in copies:
            copy.start()
        for copy in copies:
            copy.wait()
        out[0], out[1] = grams(rows, [block], act_width, grad_width)

    @pl.when(core != turn)
    def _():
        out[...] = before[...]


def gram_kernel(act_width, grad_width, rows, partner, stack, *refs):
    late, (kept, sent, hot) = refs[:-3], refs[-3:]
    blocks = [stack.at[i] for i in range(stack.shape[0])] + list(late)
    mirrored = [blocks[i] for i in MIRROR]
    sent[0], sent[1] = grams(partner, mirrored, act_width, grad_width)
    kept[0], kept[1] = grams(rows, blocks[1:], act_width, grad_width)
    hot[...] = val_onehot(blocks)


def score_kernel(ids, first, kept, came, hot, out):
    split, by_val = first.shape[2], 0.0
    for own, there in ((first, slice(0, split)), (kept, slice(split, hot.shape[0]))):
        product = (own[0] + came[0][:, there]) * (own[1] + came[1][:, there])
        by_val = by_val + jnp.dot(
            product, hot[there, :], precision=HIGHEST, preferred_element_type=F32
        )
    places = lax.broadcasted_iota(jnp.int32, (SEQ_DEV, ids.shape[1]), 0)
    onehot = (ids[...] == places).astype(F32)
    out[...] = jnp.dot(onehot, by_val, precision=HIGHEST, preferred_element_type=F32)


def call(kernel, spaces, shapes, operands, mebibytes, scratch=(), flops=0):
    return pl.pallas_call(
        kernel,
        in_specs=[pl.BlockSpec(memory_space=space) for space in spaces],
        out_specs=[pl.BlockSpec(memory_space=pltpu.VMEM)] * len(shapes),
        out_shape=[jax.ShapeDtypeStruct(shape, dtype) for shape, dtype in shapes],
        scratch_shapes=list(scratch),
        compiler_params=pltpu.CompilerParams(vmem_limit_bytes=mebibytes * 1024 * 1024),
        cost_estimate=pl.CostEstimate(flops=flops, bytes_accessed=0, transcendentals=0),
    )(*operands)


def after(block, *done):
    return lax.optimization_barrier((block, *done))[0]


def on_device(train_acts, train_grads, train_ids, val_acts, val_grads, val_ids):
    tokens = train_acts.shape[1]
    act_width, grad_width = train_acts.shape[2] // 2, train_grads.shape[2] // 2
    both = ("zy", "core")
    places = lax.axis_size("zy") * 2
    sections = lax.axis_size("section")
    core = lax.axis_index("core")

    def mover(target):
        pairs = [(i, target(i) % places) for i in range(places)]
        return lambda block: lax.ppermute(block, both, pairs)

    ahead = mover(lambda i: i + 4 if i % 2 == 0 else i - 4)
    back = mover(lambda i: i - 4 if i % 2 == 0 else i + 4)
    beside = mover(lambda i: i ^ 2)
    other_core = mover(lambda i: i ^ 1)

    def columns(acts, grads, which):
        return [
            lax.dynamic_slice_in_dim(acts[0], which * act_width, act_width, 1),
            lax.dynamic_slice_in_dim(grads[0], which * grad_width, grad_width, 1),
        ]

    numbers = jnp.broadcast_to(val_ids.astype(jnp.bfloat16)[:, None], (SEQ_DEV, LANES))
    mine = jnp.concatenate([*columns(val_acts, val_grads, core), numbers], axis=1)
    theirs = jnp.concatenate([*columns(val_acts, val_grads, 1 - core), numbers], axis=1)
    own, other = {}, {}
    other_grads = other_core(train_grads)
    came = other_core(after(theirs, other_grads))
    first = core == 0
    own[0] = jnp.concatenate(
        [jnp.where(first, mine, came), jnp.where(first, came, mine)], axis=0
    )

    widths = (act_width, grad_width)
    first_shape = ((2, tokens, own[0].shape[0]), F32)

    def first_grams(turn, before):
        return call(
            functools.partial(first_kernel, turn, *widths),
            [pltpu.SMEM] + [pltpu.HBM] * 2 + [pltpu.VMEM] * 2,
            [first_shape],
            [core.reshape(1), train_acts, train_grads, own[0], before],
            FIRST_MIB,
            [
                pltpu.VMEM((tokens, act_width + grad_width), train_acts.dtype),
                pltpu.SemaphoreType.DMA((2,)),
            ],
        )[0]

    other_acts = other_core(after(train_acts, own[0]))
    nothing = jnp.zeros(*first_shape)
    own[0], grams_before = lax.optimization_barrier((own[0], first_grams(1, nothing)))
    own[-1] = ahead(own[0])
    other[0] = beside(own[0])
    own[1] = back(own[0])
    own[-2] = ahead(own[-1])
    other[1] = beside(own[1])
    own[2] = back(after(own[1], other[0]))
    own[-3] = ahead(own[-2])
    other[-2] = beside(after(own[-2], other[0]))
    other[2] = back(after(other[1], own[2]))
    own[4] = ahead(own[-3])
    other[-3] = beside(after(own[-3], other[1]))
    own[3] = back(after(own[2], other[2], other[-2]))
    grams_first = first_grams(0, after(grams_before, own[-2], own[2], other[1]))
    late = [
        beside(after(own[4], other[-2])),
        ahead(after(other[0], own[4])),
        back(after(other[2], own[3], other[-3], grams_first)),
    ]
    early = [own[d] for d in (0, -1, 1, -2, 2, -3, 3, 4)] + [other[d] for d in (0, -2, 2, 1, -3)]

    vmem, hbm = pltpu.VMEM, pltpu.HBM
    cost = 4 * tokens * 256 * (act_width + grad_width)
    rows_shape = ((tokens, act_width + grad_width), train_acts.dtype)

    stack_shape = ((len(early), *own[0].shape), own[0].dtype)
    gram_shape = ((2, tokens, len(MIRROR) * own[0].shape[0]), F32)
    kept_shape = ((2, tokens, (len(MIRROR) - 1) * own[0].shape[0]), F32)
    hot_shape = ((len(MIRROR) * own[0].shape[0], VAL_SEQS), F32)
    rows, partner, stack = call(
        functools.partial(fetch_kernel, *widths),
        [pltpu.SMEM] + [hbm] * (4 + len(early)),
        [rows_shape, rows_shape, stack_shape],
        [core.reshape(1), train_acts, train_grads, other_acts, other_grads, *early],
        FETCH_MIB,
        [pltpu.SemaphoreType.DMA((2, 2)), pltpu.SemaphoreType.DMA((len(early),))],
    )
    kept, sent, hot = call(
        functools.partial(gram_kernel, *widths),
        [vmem] * (3 + len(late)),
        [kept_shape, gram_shape, hot_shape],
        [rows, partner, stack, *late],
        LATE_MIB,
        (),
        cost,
    )
    local_ids = train_ids - (lax.axis_index("zy") * 2 + core) * SEQ_DEV
    operands = [local_ids[None, :], grams_first, kept, other_core(sent), hot]
    (score,) = call(
        score_kernel, [vmem] * len(operands), [((SEQ_DEV, VAL_SEQS), F32)], operands, LATE_MIB
    )
    share = VAL_SEQS // sections
    parts = score.reshape(SEQ_DEV, sections, share).transpose(1, 0, 2)
    return jnp.sum(lax.all_to_all(parts, "section", 0, 0, tiled=True), axis=0)


def solution(mesh):
    cores = 2
    sections, rest = mesh.devices.shape
    grid = Mesh(mesh.devices.reshape(sections, rest // cores, cores), ("section", "zy", "core"))
    both = ("zy", "core")
    return jax.shard_map(
        on_device,
        mesh=grid,
        in_specs=(
            P("section", both, None),
            P("section", both, None),
            P(both),
            P("section", both, None),
            P("section", both, None),
            P(both),
        ),
        out_specs=P(both, "section"),
        check_vma=False,
    )
```

```python
import functools

import jax
import jax.numpy as jnp
from jax import lax
from jax.experimental import pallas as pl
from jax.experimental.pallas import tpu as pltpu
from jax.sharding import Mesh, PartitionSpec as P

SEQ_DEV = 8
VAL_SEQS = 16
LANES = 128
ACT_TILES = 2
FETCH_MIB = 22
LATE_MIB = 8
MIRROR = (0, 2, 1, 4, 3, 6, 5, 7, 8, 10, 9, 14, 15, 13, 11, 12)
F32 = jnp.float32
HIGHEST = lax.Precision.HIGHEST


def contract(left, piece):
    return lax.dot_general(left, piece, (((1,), (1,)), ((), ())), preferred_element_type=F32)


def grams(train, blocks, act_width, grad_width):
    tile = act_width // ACT_TILES
    starts = [(i * tile, tile) for i in range(ACT_TILES)] + [(act_width, grad_width)]
    parts = []
    for start, size in starts:
        piece = jnp.concatenate([block[:, start : start + size] for block in blocks], axis=0)
        parts.append(contract(train[:, start : start + size], piece))
    return sum(parts[1:-1], parts[0]), parts[-1]


def val_onehot(blocks):
    width = blocks[0].shape[1]
    numbers = [block[:, width - LANES :].astype(F32)[:, :VAL_SEQS] for block in blocks]
    stacked = jnp.concatenate(numbers, axis=0)
    return (stacked == lax.broadcasted_iota(jnp.int32, stacked.shape, 1).astype(F32)).astype(F32)


def fetch_kernel(act_width, grad_width, *refs):
    core, sources = refs[0][0], (refs[1:3], refs[3:5])
    blocks, (own, partner, stack, sems, val_sems) = refs[5:-5], refs[-5:]
    copies = [
        pltpu.make_async_copy(block, stack.at[i], val_sems.at[i]) for i, block in enumerate(blocks)
    ]
    for k, (pair, target) in enumerate(zip(sources, (own, partner))):
        begin = 0
        for j, (source, size) in enumerate(zip(pair, (act_width, grad_width))):
            held = source.at[0, :, pl.ds(pl.multiple_of(core * size, LANES), size)]
            copies.append(
                pltpu.make_async_copy(held, target.at[:, begin : begin + size], sems.at[k, j])
            )
            begin += size
    for copy in copies:
        copy.start()
    for copy in copies:
        copy.wait()


def gram_kernel(act_width, grad_width, rows, partner, stack, *refs):
    late, (kept, sent, hot) = refs[:-3], refs[-3:]
    blocks = [stack.at[i] for i in range(stack.shape[0])] + list(late)
    mirrored = [blocks[i] for i in MIRROR]
    sent[0], sent[1] = grams(partner, mirrored, act_width, grad_width)
    kept[0], kept[1] = grams(rows, blocks, act_width, grad_width)
    hot[...] = val_onehot(blocks)


def score_kernel(ids, kept, came, hot, out):
    product = (kept[0] + came[0]) * (kept[1] + came[1])
    by_val = jnp.dot(product, hot[...], precision=HIGHEST, preferred_element_type=F32)
    places = lax.broadcasted_iota(jnp.int32, (SEQ_DEV, ids.shape[1]), 0)
    onehot = (ids[...] == places).astype(F32)
    out[...] = jnp.dot(onehot, by_val, precision=HIGHEST, preferred_element_type=F32)


def call(kernel, spaces, shapes, operands, mebibytes, scratch=(), flops=0):
    return pl.pallas_call(
        kernel,
        in_specs=[pl.BlockSpec(memory_space=space) for space in spaces],
        out_specs=[pl.BlockSpec(memory_space=pltpu.VMEM)] * len(shapes),
        out_shape=[jax.ShapeDtypeStruct(shape, dtype) for shape, dtype in shapes],
        scratch_shapes=list(scratch),
        compiler_params=pltpu.CompilerParams(vmem_limit_bytes=mebibytes * 1024 * 1024),
        cost_estimate=pl.CostEstimate(flops=flops, bytes_accessed=0, transcendentals=0),
    )(*operands)


def after(block, *done):
    return lax.optimization_barrier((block, *done))[0]


def on_device(train_acts, train_grads, train_ids, val_acts, val_grads, val_ids):
    tokens = train_acts.shape[1]
    act_width, grad_width = train_acts.shape[2] // 2, train_grads.shape[2] // 2
    both = ("zy", "core")
    places = lax.axis_size("zy") * 2
    sections = lax.axis_size("section")
    core = lax.axis_index("core")

    def mover(target):
        pairs = [(i, target(i) % places) for i in range(places)]
        return lambda block: lax.ppermute(block, both, pairs)

    ahead = mover(lambda i: i + 4 if i % 2 == 0 else i - 4)
    back = mover(lambda i: i - 4 if i % 2 == 0 else i + 4)
    beside = mover(lambda i: i ^ 2)
    other_core = mover(lambda i: i ^ 1)

    def columns(acts, grads, which):
        return [
            lax.dynamic_slice_in_dim(acts[0], which * act_width, act_width, 1),
            lax.dynamic_slice_in_dim(grads[0], which * grad_width, grad_width, 1),
        ]

    numbers = jnp.broadcast_to(val_ids.astype(jnp.bfloat16)[:, None], (SEQ_DEV, LANES))
    mine = jnp.concatenate([*columns(val_acts, val_grads, core), numbers], axis=1)
    theirs = jnp.concatenate([*columns(val_acts, val_grads, 1 - core), numbers], axis=1)
    own, other = {}, {}
    other_grads = other_core(train_grads)
    came = other_core(after(theirs, other_grads))
    first = core == 0
    own[0] = jnp.concatenate(
        [jnp.where(first, mine, came), jnp.where(first, came, mine)], axis=0
    )

    other_acts = other_core(after(train_acts, own[0]))
    own[-1] = ahead(own[0])
    other[0] = beside(own[0])
    own[1] = back(own[0])
    own[-2] = ahead(after(own[-1], other[0]))
    other[1] = beside(own[1])
    own[2] = back(own[1])
    own[-3] = ahead(own[-2])
    other[-2] = beside(after(own[-2], other[0]))
    own[3] = back(own[2])
    own[4] = ahead(after(own[-3], other[1]))
    other[-3] = beside(after(own[-3], other[1]))
    other[2] = back(after(other[1], own[3]))
    late = [
        beside(after(own[4], other[-2])),
        ahead(after(other[0], own[4], other[-2])),
        back(after(other[2], other[-3])),
    ]
    early = [own[d] for d in (0, -1, 1, -2, 2, -3, 3, 4)] + [other[d] for d in (0, -2, 2, 1, -3)]

    vmem, hbm = pltpu.VMEM, pltpu.HBM
    cost = 4 * tokens * 256 * (act_width + grad_width)
    rows_shape = ((tokens, act_width + grad_width), train_acts.dtype)

    widths = (act_width, grad_width)
    stack_shape = ((len(early), *own[0].shape), own[0].dtype)
    gram_shape = ((2, tokens, len(MIRROR) * own[0].shape[0]), F32)
    hot_shape = ((len(MIRROR) * own[0].shape[0], VAL_SEQS), F32)
    rows, partner, stack = call(
        functools.partial(fetch_kernel, *widths),
        [pltpu.SMEM] + [hbm] * (4 + len(early)),
        [rows_shape, rows_shape, stack_shape],
        [core.reshape(1), train_acts, train_grads, other_acts, other_grads, *early],
        FETCH_MIB,
        [pltpu.SemaphoreType.DMA((2, 2)), pltpu.SemaphoreType.DMA((len(early),))],
    )
    kept, sent, hot = call(
        functools.partial(gram_kernel, *widths),
        [vmem] * (3 + len(late)),
        [gram_shape, gram_shape, hot_shape],
        [rows, partner, stack, *late],
        LATE_MIB,
        (),
        cost,
    )
    local_ids = train_ids - (lax.axis_index("zy") * 2 + core) * SEQ_DEV
    operands = [local_ids[None, :], kept, other_core(sent), hot]
    (score,) = call(
        score_kernel, [vmem] * len(operands), [((SEQ_DEV, VAL_SEQS), F32)], operands, LATE_MIB
    )
    share = VAL_SEQS // sections
    parts = score.reshape(SEQ_DEV, sections, share).transpose(1, 0, 2)
    return jnp.sum(lax.all_to_all(parts, "section", 0, 0, tiled=True), axis=0)


def solution(mesh):
    cores = 2
    sections, rest = mesh.devices.shape
    grid = Mesh(mesh.devices.reshape(sections, rest // cores, cores), ("section", "zy", "core"))
    both = ("zy", "core")
    return jax.shard_map(
        on_device,
        mesh=grid,
        in_specs=(
            P("section", both, None),
            P("section", both, None),
            P(both),
            P("section", both, None),
            P("section", both, None),
            P(both),
        ),
        out_specs=P(both, "section"),
        check_vma=False,
    )
```

```python
import functools

import jax
import jax.numpy as jnp
from jax import lax
from jax.experimental import pallas as pl
from jax.experimental.pallas import tpu as pltpu
from jax.sharding import Mesh, PartitionSpec as P

SEQ_DEV = 8
VAL_SEQS = 16
LANES = 128
ACT_TILES = 1
FETCH_MIB = 22
LATE_MIB = 8
MIRROR = (0, 2, 1, 4, 3, 6, 5, 7, 8, 10, 9, 14, 15, 13, 11, 12)
F32 = jnp.float32
HIGHEST = lax.Precision.HIGHEST


def contract(left, piece):
    return lax.dot_general(left, piece, (((1,), (1,)), ((), ())), preferred_element_type=F32)


def grams(train, blocks, act_width, grad_width):
    tile = act_width // ACT_TILES
    starts = [(i * tile, tile) for i in range(ACT_TILES)] + [(act_width, grad_width)]
    parts = []
    for start, size in starts:
        piece = jnp.concatenate([block[:, start : start + size] for block in blocks], axis=0)
        parts.append(contract(train[:, start : start + size], piece))
    return sum(parts[1:-1], parts[0]), parts[-1]


def val_onehot(blocks):
    width = blocks[0].shape[1]
    numbers = [block[:, width - LANES :].astype(F32)[:, :VAL_SEQS] for block in blocks]
    stacked = jnp.concatenate(numbers, axis=0)
    return (stacked == lax.broadcasted_iota(jnp.int32, stacked.shape, 1).astype(F32)).astype(F32)


def fetch_kernel(act_width, grad_width, *refs):
    core, sources = refs[0][0], (refs[1:3], refs[3:5])
    blocks, (own, partner, stack, sems, val_sems) = refs[5:-5], refs[-5:]
    copies = [
        pltpu.make_async_copy(block, stack.at[i], val_sems.at[i]) for i, block in enumerate(blocks)
    ]
    for k, (pair, target) in enumerate(zip(sources, (own, partner))):
        begin = 0
        for j, (source, size) in enumerate(zip(pair, (act_width, grad_width))):
            held = source.at[0, :, pl.ds(pl.multiple_of(core * size, LANES), size)]
            copies.append(
                pltpu.make_async_copy(held, target.at[:, begin : begin + size], sems.at[k, j])
            )
            begin += size
    for copy in copies:
        copy.start()
    for copy in copies:
        copy.wait()


def gram_kernel(act_width, grad_width, rows, partner, stack, *refs):
    late, (kept, sent, hot) = refs[:-3], refs[-3:]
    blocks = [stack.at[i] for i in range(stack.shape[0])] + list(late)
    mirrored = [blocks[i] for i in MIRROR]
    sent[0], sent[1] = grams(partner, mirrored, act_width, grad_width)
    kept[0], kept[1] = grams(rows, blocks, act_width, grad_width)
    hot[...] = val_onehot(blocks)


def score_kernel(ids, kept, came, hot, out):
    product = (kept[0] + came[0]) * (kept[1] + came[1])
    by_val = jnp.dot(product, hot[...], precision=HIGHEST, preferred_element_type=F32)
    places = lax.broadcasted_iota(jnp.int32, (SEQ_DEV, ids.shape[1]), 0)
    onehot = (ids[...] == places).astype(F32)
    out[...] = jnp.dot(onehot, by_val, precision=HIGHEST, preferred_element_type=F32)


def call(kernel, spaces, shapes, operands, mebibytes, scratch=(), flops=0):
    return pl.pallas_call(
        kernel,
        in_specs=[pl.BlockSpec(memory_space=space) for space in spaces],
        out_specs=[pl.BlockSpec(memory_space=pltpu.VMEM)] * len(shapes),
        out_shape=[jax.ShapeDtypeStruct(shape, dtype) for shape, dtype in shapes],
        scratch_shapes=list(scratch),
        compiler_params=pltpu.CompilerParams(vmem_limit_bytes=mebibytes * 1024 * 1024),
        cost_estimate=pl.CostEstimate(flops=flops, bytes_accessed=0, transcendentals=0),
    )(*operands)


def after(block, *done):
    return lax.optimization_barrier((block, *done))[0]


def on_device(train_acts, train_grads, train_ids, val_acts, val_grads, val_ids):
    tokens = train_acts.shape[1]
    act_width, grad_width = train_acts.shape[2] // 2, train_grads.shape[2] // 2
    both = ("zy", "core")
    places = lax.axis_size("zy") * 2
    sections = lax.axis_size("section")
    core = lax.axis_index("core")

    def mover(target):
        pairs = [(i, target(i) % places) for i in range(places)]
        return lambda block: lax.ppermute(block, both, pairs)

    ahead = mover(lambda i: i + 4 if i % 2 == 0 else i - 4)
    back = mover(lambda i: i - 4 if i % 2 == 0 else i + 4)
    beside = mover(lambda i: i ^ 2)
    other_core = mover(lambda i: i ^ 1)

    def columns(acts, grads, which):
        return [
            lax.dynamic_slice_in_dim(acts[0], which * act_width, act_width, 1),
            lax.dynamic_slice_in_dim(grads[0], which * grad_width, grad_width, 1),
        ]

    numbers = jnp.broadcast_to(val_ids[:, None], (SEQ_DEV, LANES)).astype(jnp.bfloat16)
    mine = jnp.concatenate([*columns(val_acts, val_grads, core), numbers], axis=1)
    theirs = jnp.concatenate([*columns(val_acts, val_grads, 1 - core), numbers], axis=1)
    own, other = {}, {}
    other_grads = other_core(train_grads)
    came = other_core(after(theirs, other_grads))
    first = core == 0
    own[0] = jnp.concatenate(
        [jnp.where(first, mine, came), jnp.where(first, came, mine)], axis=0
    )

    other_acts = other_core(after(train_acts, own[0]))
    own[-1] = ahead(own[0])
    other[0] = beside(own[0])
    own[1] = back(own[0])
    own[-2] = ahead(after(own[-1], other[0]))
    other[1] = beside(own[1])
    own[2] = back(own[1])
    own[-3] = ahead(own[-2])
    other[-2] = beside(after(own[-2], other[0]))
    own[3] = back(own[2])
    own[4] = ahead(after(own[-3], other[1]))
    other[-3] = beside(after(own[-3], other[1]))
    other[2] = back(after(other[1], own[3]))
    late = [
        beside(after(own[4], other[-2])),
        ahead(after(other[0], own[4], other[-2])),
        back(after(other[2], other[-3])),
    ]
    early = [own[d] for d in (0, -1, 1, -2, 2, -3, 3, 4)] + [other[d] for d in (0, -2, 2, 1, -3)]

    vmem, hbm = pltpu.VMEM, pltpu.HBM
    cost = 4 * tokens * 256 * (act_width + grad_width)
    rows_shape = ((tokens, act_width + grad_width), train_acts.dtype)

    widths = (act_width, grad_width)
    stack_shape = ((len(early), *own[0].shape), own[0].dtype)
    gram_shape = ((2, tokens, len(MIRROR) * own[0].shape[0]), F32)
    hot_shape = ((len(MIRROR) * own[0].shape[0], VAL_SEQS), F32)
    rows, partner, stack = call(
        functools.partial(fetch_kernel, *widths),
        [pltpu.SMEM] + [hbm] * (4 + len(early)),
        [rows_shape, rows_shape, stack_shape],
        [core.reshape(1), train_acts, train_grads, other_acts, other_grads, *early],
        FETCH_MIB,
        [pltpu.SemaphoreType.DMA((2, 2)), pltpu.SemaphoreType.DMA((len(early),))],
    )
    kept, sent, hot = call(
        functools.partial(gram_kernel, *widths),
        [vmem] * (3 + len(late)),
        [gram_shape, gram_shape, hot_shape],
        [rows, partner, stack, *late],
        LATE_MIB,
        (),
        cost,
    )
    local_ids = train_ids - (lax.axis_index("zy") * 2 + core) * SEQ_DEV
    operands = [local_ids[None, :], kept, other_core(sent), hot]
    (score,) = call(
        score_kernel, [vmem] * len(operands), [((SEQ_DEV, VAL_SEQS), F32)], operands, LATE_MIB
    )
    share = VAL_SEQS // sections
    parts = score.reshape(SEQ_DEV, sections, share).transpose(1, 0, 2)
    return jnp.sum(lax.all_to_all(parts, "section", 0, 0, tiled=True), axis=0)


def solution(mesh):
    cores = 2
    sections, rest = mesh.devices.shape
    grid = Mesh(mesh.devices.reshape(sections, rest // cores, cores), ("section", "zy", "core"))
    both = ("zy", "core")
    return jax.shard_map(
        on_device,
        mesh=grid,
        in_specs=(
            P("section", both, None),
            P("section", both, None),
            P(both),
            P("section", both, None),
            P("section", both, None),
            P(both),
        ),
        out_specs=P(both, "section"),
        check_vma=False,
    )
```

```python
import functools

import jax
import jax.numpy as jnp
from jax import lax
from jax.experimental import pallas as pl
from jax.experimental.pallas import tpu as pltpu
from jax.sharding import Mesh, PartitionSpec as P

SEQ_DEV = 8
VAL_SEQS = 16
LANES = 128
ACT_TILES = 1
FETCH_MIB = 22
LATE_MIB = 8
MIRROR = (0, 2, 1, 4, 3, 6, 5, 7, 8, 10, 9, 14, 15, 13, 11, 12)
F32 = jnp.float32
HIGHEST = lax.Precision.HIGHEST


def contract(left, piece):
    return lax.dot_general(left, piece, (((1,), (1,)), ((), ())), preferred_element_type=F32)


def grams(train, blocks, act_width, grad_width):
    tile = act_width // ACT_TILES
    starts = [(i * tile, tile) for i in range(ACT_TILES)] + [(act_width, grad_width)]
    parts = []
    for start, size in starts:
        piece = jnp.concatenate([block[:, start : start + size] for block in blocks], axis=0)
        parts.append(contract(train[:, start : start + size], piece))
    return sum(parts[1:-1], parts[0]), parts[-1]


def val_onehot(blocks):
    width = blocks[0].shape[1]
    numbers = [block[:, width - LANES :].astype(F32)[:, :VAL_SEQS] for block in blocks]
    stacked = jnp.concatenate(numbers, axis=0)
    return (stacked == lax.broadcasted_iota(jnp.int32, stacked.shape, 1).astype(F32)).astype(F32)


def fetch_kernel(act_width, grad_width, *refs):
    core, sources = refs[0][0], (refs[1:3], refs[3:5])
    blocks, (own, partner, stack, sems, val_sems) = refs[5:-5], refs[-5:]
    copies = [
        pltpu.make_async_copy(block, stack.at[i], val_sems.at[i]) for i, block in enumerate(blocks)
    ]
    for k, (pair, target) in enumerate(zip(sources, (own, partner))):
        begin = 0
        for j, (source, size) in enumerate(zip(pair, (act_width, grad_width))):
            held = source.at[0, :, pl.ds(pl.multiple_of(core * size, LANES), size)]
            copies.append(
                pltpu.make_async_copy(held, target.at[:, begin : begin + size], sems.at[k, j])
            )
            begin += size
    for copy in copies:
        copy.start()
    for copy in copies:
        copy.wait()


def gram_kernel(act_width, grad_width, rows, partner, stack, *refs):
    late, (kept, sent, hot) = refs[:-3], refs[-3:]
    blocks = [stack.at[i] for i in range(stack.shape[0])] + list(late)
    mirrored = [blocks[i] for i in MIRROR]
    sent[0], sent[1] = grams(partner, mirrored, act_width, grad_width)
    kept[0], kept[1] = grams(rows, blocks, act_width, grad_width)
    hot[...] = val_onehot(blocks)


def score_kernel(ids, kept, came, hot, out):
    product = (kept[0] + came[0]) * (kept[1] + came[1])
    by_val = jnp.dot(product, hot[...], precision=HIGHEST, preferred_element_type=F32)
    places = lax.broadcasted_iota(jnp.int32, (SEQ_DEV, ids.shape[1]), 0)
    onehot = (ids[...] == places).astype(F32)
    out[...] = jnp.dot(onehot, by_val, precision=HIGHEST, preferred_element_type=F32)


def call(kernel, spaces, shapes, operands, mebibytes, scratch=(), flops=0):
    return pl.pallas_call(
        kernel,
        in_specs=[pl.BlockSpec(memory_space=space) for space in spaces],
        out_specs=[pl.BlockSpec(memory_space=pltpu.VMEM)] * len(shapes),
        out_shape=[jax.ShapeDtypeStruct(shape, dtype) for shape, dtype in shapes],
        scratch_shapes=list(scratch),
        compiler_params=pltpu.CompilerParams(vmem_limit_bytes=mebibytes * 1024 * 1024),
        cost_estimate=pl.CostEstimate(flops=flops, bytes_accessed=0, transcendentals=0),
    )(*operands)


def after(block, *done):
    return lax.optimization_barrier((block, *done))[0]


def on_device(train_acts, train_grads, train_ids, val_acts, val_grads, val_ids):
    tokens = train_acts.shape[1]
    act_width, grad_width = train_acts.shape[2] // 2, train_grads.shape[2] // 2
    both = ("zy", "core")
    places = lax.axis_size("zy") * 2
    sections = lax.axis_size("section")
    core = lax.axis_index("core")

    def mover(target):
        pairs = [(i, target(i) % places) for i in range(places)]
        return lambda block: lax.ppermute(block, both, pairs)

    ahead = mover(lambda i: i + 4 if i % 2 == 0 else i - 4)
    back = mover(lambda i: i - 4 if i % 2 == 0 else i + 4)
    beside = mover(lambda i: i ^ 2)
    other_core = mover(lambda i: i ^ 1)

    def columns(acts, grads, which):
        return [
            lax.dynamic_slice_in_dim(acts[0], which * act_width, act_width, 1),
            lax.dynamic_slice_in_dim(grads[0], which * grad_width, grad_width, 1),
        ]

    numbers = jnp.broadcast_to(val_ids[:, None], (SEQ_DEV, LANES)).astype(jnp.bfloat16)
    mine = jnp.concatenate([*columns(val_acts, val_grads, core), numbers], axis=1)
    theirs = jnp.concatenate([*columns(val_acts, val_grads, 1 - core), numbers], axis=1)
    own, other = {}, {}
    came = other_core(theirs)
    first = core == 0
    own[0] = jnp.concatenate(
        [jnp.where(first, mine, came), jnp.where(first, came, mine)], axis=0
    )

    other_grads = other_core(after(train_grads, own[0]))
    other_acts = other_core(after(train_acts, own[0]))
    own[-1] = ahead(own[0])
    other[0] = beside(own[0])
    own[1] = back(after(own[0], other_grads))
    own[-2] = ahead(after(own[-1], other[0]))
    other[1] = beside(own[1])
    own[2] = back(own[1])
    own[-3] = ahead(own[-2])
    other[-2] = beside(after(own[-2], other[0]))
    own[3] = back(own[2])
    own[4] = ahead(after(own[-3], other[1]))
    other[-3] = beside(after(own[-3], other[1]))
    other[2] = back(after(other[1], own[3]))
    late = [
        beside(after(own[4], other[-2])),
        ahead(after(other[0], own[4], other[-2])),
        back(after(other[2], other[-3])),
    ]
    early = [own[d] for d in (0, -1, 1, -2, 2, -3, 3, 4)] + [other[d] for d in (0, -2, 2, 1, -3)]

    vmem, hbm = pltpu.VMEM, pltpu.HBM
    cost = 4 * tokens * 256 * (act_width + grad_width)
    rows_shape = ((tokens, act_width + grad_width), train_acts.dtype)

    widths = (act_width, grad_width)
    stack_shape = ((len(early), *own[0].shape), own[0].dtype)
    gram_shape = ((2, tokens, len(MIRROR) * own[0].shape[0]), F32)
    hot_shape = ((len(MIRROR) * own[0].shape[0], VAL_SEQS), F32)
    rows, partner, stack = call(
        functools.partial(fetch_kernel, *widths),
        [pltpu.SMEM] + [hbm] * (4 + len(early)),
        [rows_shape, rows_shape, stack_shape],
        [core.reshape(1), train_acts, train_grads, other_acts, other_grads, *early],
        FETCH_MIB,
        [pltpu.SemaphoreType.DMA((2, 2)), pltpu.SemaphoreType.DMA((len(early),))],
    )
    kept, sent, hot = call(
        functools.partial(gram_kernel, *widths),
        [vmem] * (3 + len(late)),
        [gram_shape, gram_shape, hot_shape],
        [rows, partner, stack, *late],
        LATE_MIB,
        (),
        cost,
    )
    local_ids = train_ids - (lax.axis_index("zy") * 2 + core) * SEQ_DEV
    operands = [local_ids[None, :], kept, other_core(sent), hot]
    (score,) = call(
        score_kernel, [vmem] * len(operands), [((SEQ_DEV, VAL_SEQS), F32)], operands, LATE_MIB
    )
    share = VAL_SEQS // sections
    parts = score.reshape(SEQ_DEV, sections, share).transpose(1, 0, 2)
    return jnp.sum(lax.all_to_all(parts, "section", 0, 0, tiled=True), axis=0)


def solution(mesh):
    cores = 2
    sections, rest = mesh.devices.shape
    grid = Mesh(mesh.devices.reshape(sections, rest // cores, cores), ("section", "zy", "core"))
    both = ("zy", "core")
    return jax.shard_map(
        on_device,
        mesh=grid,
        in_specs=(
            P("section", both, None),
            P("section", both, None),
            P(both),
            P("section", both, None),
            P("section", both, None),
            P(both),
        ),
        out_specs=P(both, "section"),
        check_vma=False,
    )
```

```python
import functools

import jax
import jax.numpy as jnp
from jax import lax
from jax.experimental import pallas as pl
from jax.experimental.pallas import tpu as pltpu
from jax.sharding import Mesh, PartitionSpec as P

SEQ_DEV = 8
VAL_SEQS = 16
LANES = 128
ACT_TILES = 1
FETCH_MIB = 22
LATE_MIB = 8
MIRROR = (0, 2, 1, 4, 3, 6, 5, 7, 8, 10, 9, 14, 15, 13, 11, 12)
F32 = jnp.float32
HIGHEST = lax.Precision.HIGHEST


def contract(left, piece):
    return lax.dot_general(left, piece, (((1,), (1,)), ((), ())), preferred_element_type=F32)


def grams(train, blocks, act_width, grad_width):
    tile = act_width // ACT_TILES
    starts = [(i * tile, tile) for i in range(ACT_TILES)] + [(act_width, grad_width)]
    parts = []
    for start, size in starts:
        piece = jnp.concatenate([block[:, start : start + size] for block in blocks], axis=0)
        parts.append(contract(train[:, start : start + size], piece))
    return sum(parts[1:-1], parts[0]), parts[-1]


def val_onehot(blocks):
    width = blocks[0].shape[1]
    numbers = [block[:, width - LANES :].astype(F32)[:, :VAL_SEQS] for block in blocks]
    stacked = jnp.concatenate(numbers, axis=0)
    return (stacked == lax.broadcasted_iota(jnp.int32, stacked.shape, 1).astype(F32)).astype(F32)


def fetch_kernel(act_width, grad_width, *refs):
    core, sources = refs[0][0], (refs[1:3], refs[3:5])
    blocks, (own, partner, stack, sems, val_sems) = refs[5:-5], refs[-5:]
    copies = [
        pltpu.make_async_copy(block, stack.at[i], val_sems.at[i]) for i, block in enumerate(blocks)
    ]
    for k, (pair, target) in enumerate(zip(sources, (own, partner))):
        begin = 0
        for j, (source, size) in enumerate(zip(pair, (act_width, grad_width))):
            held = source.at[0, :, pl.ds(pl.multiple_of(core * size, LANES), size)]
            copies.append(
                pltpu.make_async_copy(held, target.at[:, begin : begin + size], sems.at[k, j])
            )
            begin += size
    for copy in copies:
        copy.start()
    for copy in copies:
        copy.wait()


def gram_kernel(act_width, grad_width, rows, partner, stack, *refs):
    late, (kept, sent, hot) = refs[:-3], refs[-3:]
    blocks = [stack.at[i] for i in range(stack.shape[0])] + list(late)
    mirrored = [blocks[i] for i in MIRROR]
    sent[0], sent[1] = grams(partner, mirrored, act_width, grad_width)
    kept[0], kept[1] = grams(rows, blocks, act_width, grad_width)
    hot[...] = val_onehot(blocks)


def score_kernel(ids, kept, came, hot, out):
    product = (kept[0] + came[0]) * (kept[1] + came[1])
    by_val = jnp.dot(product, hot[...], precision=HIGHEST, preferred_element_type=F32)
    places = lax.broadcasted_iota(jnp.int32, (SEQ_DEV, ids.shape[1]), 0)
    onehot = (ids[...] == places).astype(F32)
    out[...] = jnp.dot(onehot, by_val, precision=HIGHEST, preferred_element_type=F32)


def call(kernel, spaces, shapes, operands, mebibytes, scratch=(), flops=0):
    return pl.pallas_call(
        kernel,
        in_specs=[pl.BlockSpec(memory_space=space) for space in spaces],
        out_specs=[pl.BlockSpec(memory_space=pltpu.VMEM)] * len(shapes),
        out_shape=[jax.ShapeDtypeStruct(shape, dtype) for shape, dtype in shapes],
        scratch_shapes=list(scratch),
        compiler_params=pltpu.CompilerParams(vmem_limit_bytes=mebibytes * 1024 * 1024),
        cost_estimate=pl.CostEstimate(flops=flops, bytes_accessed=0, transcendentals=0),
    )(*operands)


def after(block, *done):
    return lax.optimization_barrier((block, *done))[0]


def on_device(train_acts, train_grads, train_ids, val_acts, val_grads, val_ids):
    tokens = train_acts.shape[1]
    act_width, grad_width = train_acts.shape[2] // 2, train_grads.shape[2] // 2
    both = ("zy", "core")
    places = lax.axis_size("zy") * 2
    sections = lax.axis_size("section")
    core = lax.axis_index("core")

    def mover(target):
        pairs = [(i, target(i) % places) for i in range(places)]
        return lambda block: lax.ppermute(block, both, pairs)

    ahead = mover(lambda i: i + 4 if i % 2 == 0 else i - 4)
    back = mover(lambda i: i - 4 if i % 2 == 0 else i + 4)
    beside = mover(lambda i: i ^ 2)
    other_core = mover(lambda i: i ^ 1)

    def columns(acts, grads, which):
        return [
            lax.dynamic_slice_in_dim(acts[0], which * act_width, act_width, 1),
            lax.dynamic_slice_in_dim(grads[0], which * grad_width, grad_width, 1),
        ]

    numbers = jnp.broadcast_to(val_ids[:, None], (SEQ_DEV, LANES)).astype(jnp.bfloat16)
    mine = jnp.concatenate([*columns(val_acts, val_grads, core), numbers], axis=1)
    theirs = jnp.concatenate([*columns(val_acts, val_grads, 1 - core), numbers], axis=1)
    own, other = {}, {}
    other_grads = other_core(train_grads)
    came = other_core(after(theirs, other_grads))
    first = core == 0
    own[0] = jnp.concatenate(
        [jnp.where(first, mine, came), jnp.where(first, came, mine)], axis=0
    )

    other_acts = other_core(after(train_acts, own[0]))
    own[-1] = ahead(own[0])
    other[0] = beside(own[0])
    own[1] = back(own[0])
    own[-2] = ahead(own[-1])
    other[1] = beside(own[1])
    own[2] = back(own[1])
    own[-3] = ahead(after(own[-2], other[0]))
    other[-2] = beside(after(own[-2], other[0]))
    own[3] = back(own[2])
    own[4] = ahead(after(own[-3], other[1]))
    other[-3] = beside(after(own[-3], other[1]))
    other[2] = back(after(other[1], own[3]))
    late = [
        beside(after(own[4], other[-2])),
        ahead(after(other[0], own[4], other[-2])),
        back(after(other[2], other[-3])),
    ]
    early = [own[d] for d in (0, -1, 1, -2, 2, -3, 3, 4)] + [other[d] for d in (0, -2, 2, 1, -3)]

    vmem, hbm = pltpu.VMEM, pltpu.HBM
    cost = 4 * tokens * 256 * (act_width + grad_width)
    rows_shape = ((tokens, act_width + grad_width), train_acts.dtype)

    widths = (act_width, grad_width)
    stack_shape = ((len(early), *own[0].shape), own[0].dtype)
    gram_shape = ((2, tokens, len(MIRROR) * own[0].shape[0]), F32)
    hot_shape = ((len(MIRROR) * own[0].shape[0], VAL_SEQS), F32)
    rows, partner, stack = call(
        functools.partial(fetch_kernel, *widths),
        [pltpu.SMEM] + [hbm] * (4 + len(early)),
        [rows_shape, rows_shape, stack_shape],
        [core.reshape(1), train_acts, train_grads, other_acts, other_grads, *early],
        FETCH_MIB,
        [pltpu.SemaphoreType.DMA((2, 2)), pltpu.SemaphoreType.DMA((len(early),))],
    )
    kept, sent, hot = call(
        functools.partial(gram_kernel, *widths),
        [vmem] * (3 + len(late)),
        [gram_shape, gram_shape, hot_shape],
        [rows, partner, stack, *late],
        LATE_MIB,
        (),
        cost,
    )
    local_ids = train_ids - (lax.axis_index("zy") * 2 + core) * SEQ_DEV
    operands = [local_ids[None, :], kept, other_core(sent), hot]
    (score,) = call(
        score_kernel, [vmem] * len(operands), [((SEQ_DEV, VAL_SEQS), F32)], operands, LATE_MIB
    )
    share = VAL_SEQS // sections
    parts = score.reshape(SEQ_DEV, sections, share).transpose(1, 0, 2)
    return jnp.sum(lax.all_to_all(parts, "section", 0, 0, tiled=True), axis=0)


def solution(mesh):
    cores = 2
    sections, rest = mesh.devices.shape
    grid = Mesh(mesh.devices.reshape(sections, rest // cores, cores), ("section", "zy", "core"))
    both = ("zy", "core")
    return jax.shard_map(
        on_device,
        mesh=grid,
        in_specs=(
            P("section", both, None),
            P("section", both, None),
            P(both),
            P("section", both, None),
            P("section", both, None),
            P(both),
        ),
        out_specs=P(both, "section"),
        check_vma=False,
    )
```
